512 devices in a mesh: dp: 64 (over z, y), tensor: 8 (over x, core).
Axes of the slice: x: 4, y: 8, z: 8, core: 2. Of those that a mesh axis runs over, the one named last changes fastest.
Arguments:
- queries: bfloat16 [16384, 3072], P(('dp', 'tensor')), may hold values from -16 to 16, as said below
- keys: bfloat16 [16384, 3072], P(('dp', 'tensor')), may hold values from -16 to 16
- values: bfloat16 [16384, 3072], P(('dp', 'tensor')), may hold values from -6 to 6
- out_grad: bfloat16 [16384, 3072], P(('dp', 'tensor')), may hold values from -6 to 6
- lengths: int32 [64, 32], replicated, may hold values from 5 to 8, as said below
- pack_of: int32 [64, 32], replicated, may hold values from 0 to 63, as said below
- source_ids: int32 [64, 32], replicated, may hold values from 0 to 7
- loss_weights: int32 [8], replicated, may hold values from 1 to 4
Outputs:
- grad_queries: bfloat16 [16384, 3072], P(('dp', 'tensor'))
- grad_keys: bfloat16 [16384, 3072], P(('dp', 'tensor'))
- grad_values: bfloat16 [16384, 3072], P(('dp', 'tensor'))
The draws below stay inside these ranges and needn't reach their ends.
Inputs may be any that keep to these rules, and one draw needn't show every extreme that they name: `queries`: queries of padding rows are drawn too. `lengths`: row s lists the patch counts of the 32 images of data index s in the order of its rows. `pack_of`: no pack receives more than one image from one data index, and every pack receives exactly 32 images.
All inputs are finite; a program needn't handle non-finite values.
Results may differ from the reference program's by a relative error of at most 0.0063.
Values may be sent and summed in bfloat16 or wider, within the bound.
No kernel may reach another device: no remote copies, remote signals or barrier semaphores. Data moves between devices by JAX's collectives and lax.ppermute only.
A program may use at most 64 MiB of HBM per device.

```python
import jax
import jax.numpy as jnp
from jax import lax

HEAD_DIM = 128
IMG_DEV = 32
PATCH_MAX = 8
SOURCES = 8
PACKS = 64
ROWS = 256
TOTAL_ROWS = 16384
FEAT = 3072


def draw_queries(key, part):
    key = jax.random.fold_in(key, 1)
    field = jax.random.normal(key, (TOTAL_ROWS, FEAT), jnp.float32)
    return jnp.clip(field, -16.0, 16.0).astype(jnp.bfloat16)


def draw_keys(key, part):
    key = jax.random.fold_in(key, 2)
    field = jax.random.normal(key, (TOTAL_ROWS, FEAT), jnp.float32)
    return jnp.clip(field, -16.0, 16.0).astype(jnp.bfloat16)


def draw_lengths(key, part):
    key = jax.random.fold_in(key, 3)
    lowest = PATCH_MAX * 5 // 8
    ceilings = jax.random.randint(jax.random.fold_in(key, 1), (PACKS, 1), PATCH_MAX * 3 // 4, PATCH_MAX + 1)
    spread = jax.random.randint(jax.random.fold_in(key, 2), (PACKS, IMG_DEV), 0, 1 << 20)
    counts = lowest + spread % (ceilings - lowest + 1)
    chosen_row = jax.random.randint(jax.random.fold_in(key, 4), (), 0, PACKS)
    chosen_col = jax.random.randint(jax.random.fold_in(key, 5), (), 0, IMG_DEV)
    other_col = (chosen_col + 1) % IMG_DEV
    row_grid = jnp.arange(PACKS, dtype=jnp.int32)[:, None]
    col_grid = jnp.arange(IMG_DEV, dtype=jnp.int32)[None, :]
    counts = jnp.where((row_grid == chosen_row) & (col_grid == chosen_col), PATCH_MAX, counts)
    counts = jnp.where((row_grid == chosen_row) & (col_grid == other_col), lowest, counts)
    return counts.astype(jnp.int32)


def draw_pack_of(key, part):
    key = jax.random.fold_in(key, 4)
    shifts = jax.random.permutation(key, PACKS).astype(jnp.int32)
    half = PACKS // 2
    first = shifts[0]
    shifts = jnp.where(shifts == half, first, shifts)
    shifts = shifts.at[0].set(half)
    picks = shifts[jnp.arange(IMG_DEV, dtype=jnp.int32) % PACKS]
    return ((jnp.arange(PACKS, dtype=jnp.int32)[:, None] + picks[None, :]) % PACKS).astype(jnp.int32)


def with_ends(result, key, least, largest):
    longest = result.shape.index(max(result.shape))
    spots = []
    for shift in (0, 1):
        where = [jax.random.randint(jax.random.fold_in(key, axis), (), 0, length) for axis, length in enumerate(result.shape)]
        where[longest] = (where[longest] + shift) % result.shape[longest]
        spots.append(tuple(where))
    return result.at[spots[0]].set(least).at[spots[1]].set(largest)


def shard_levels(key, extent, split, least, high):
    loudness, own = 1.0, jax.random.fold_in(key, 6)
    for axis_at, shards_of in split:
        heights = jnp.exp(jax.random.uniform(jax.random.fold_in(own, axis_at), (shards_of,), jnp.float32, least / len(split), high / len(split)))
        loudness = loudness * jnp.repeat(heights, extent[axis_at] // shards_of).reshape([-1 if axis == axis_at else 1 for axis in range(len(extent))])
    return loudness


def centred(rng, dims, width, bound, shards=(), kind=jnp.bfloat16):
    values = jax.random.normal(rng, dims, jnp.float32) * width
    if len(shards) > 0:
        values = shard_levels(rng, dims, shards, -0.22, 0.18) * values
    return jnp.clip(values, min=-bound, max=bound).astype(kind)


def setup_inputs(seed: int = 0) -> dict:
    seeds = jax.random.split(jax.random.key(seed), 9)
    queries = draw_queries(jax.random.fold_in(seeds[8], 71), 0)
    keys = draw_keys(jax.random.fold_in(seeds[8], 71), 0)
    values = centred(seeds[2], (TOTAL_ROWS, FEAT), 1.0, 6.0, ((0, 512),))
    out_grad = centred(seeds[3], (TOTAL_ROWS, FEAT), 1.0, 6.0, ((0, 512),))
    lengths = draw_lengths(jax.random.fold_in(seeds[8], 71), 0)
    pack_of = draw_pack_of(jax.random.fold_in(seeds[8], 71), 0)
    source_ids = with_ends(jax.random.randint(seeds[6], (PACKS, IMG_DEV), 0, SOURCES), jax.random.fold_in(seeds[6], 1), 0, SOURCES - 1).astype(jnp.int32)
    loss_weights = with_ends(jax.random.randint(seeds[7], (SOURCES,), 1, 5), jax.random.fold_in(seeds[7], 1), 1, 4).astype(jnp.int32)
    return dict(queries=queries, keys=keys, values=values, out_grad=out_grad, lengths=lengths, pack_of=pack_of, source_ids=source_ids, loss_weights=loss_weights)


MASKED = -1e30


def block_grads(queries, keys, values, grad_out, owners):
    row_count = queries.shape[0]
    score_scale = HEAD_DIM ** -0.5
    q_full = queries.reshape(row_count, -1, HEAD_DIM).astype(jnp.float32)
    k_full = keys.reshape(row_count, -1, HEAD_DIM).astype(jnp.float32)
    v_full = values.reshape(row_count, -1, HEAD_DIM).astype(jnp.float32)
    g_full = grad_out.reshape(row_count, -1, HEAD_DIM).astype(jnp.float32)
    allowed = (owners[:, None] == owners[None, :]) & (owners[:, None] >= 0)
    scores = jnp.einsum("qhd,khd->hqk", q_full, k_full, precision=lax.Precision.HIGHEST) * score_scale
    scores = jnp.where(allowed[None], scores, MASKED)
    row_max = jnp.max(scores, axis=-1, keepdims=True)
    exp_scores = jnp.exp(scores - row_max)
    soft_probs = exp_scores / jnp.sum(exp_scores, axis=-1, keepdims=True)
    soft_back = lax.optimization_barrier(soft_probs.astype(jnp.bfloat16)).astype(jnp.float32)
    attn_out = jnp.einsum("hqk,khd->qhd", soft_back, v_full, precision=lax.Precision.HIGHEST)
    row_delta = jnp.sum(g_full * attn_out, axis=-1)
    grad_values = jnp.einsum("hqk,qhd->khd", soft_back, g_full, precision=lax.Precision.HIGHEST)
    grad_probs = jnp.einsum("qhd,khd->hqk", g_full, v_full, precision=lax.Precision.HIGHEST)
    grad_scores = soft_probs * (grad_probs - jnp.transpose(row_delta)[:, :, None])
    grad_back = lax.optimization_barrier(grad_scores.astype(jnp.bfloat16)).astype(jnp.float32)
    grad_queries = jnp.einsum("hqk,khd->qhd", grad_back, k_full, precision=lax.Precision.HIGHEST) * score_scale
    grad_keys = jnp.einsum("hqk,qhd->khd", grad_back, q_full, precision=lax.Precision.HIGHEST) * score_scale
    return (grad_queries.reshape(row_count, -1).astype(jnp.bfloat16),
            grad_keys.reshape(row_count, -1).astype(jnp.bfloat16),
            grad_values.reshape(row_count, -1).astype(jnp.bfloat16))


def block_step(inputs):
    return block_grads(inputs[0], inputs[1], inputs[2], inputs[3], inputs[4])


def reference(queries, keys, values, out_grad, lengths, pack_of, source_ids, loss_weights):
    groups = lengths.shape[0]
    images = lengths.shape[1]
    row_total = ROWS
    image_ends = jnp.cumsum(lengths, axis=1).astype(jnp.int32)
    image_starts = (image_ends - lengths).astype(jnp.int32)
    row_ids = jnp.arange(row_total, dtype=jnp.int32)
    image_index = jnp.sum((row_ids[None, :, None] >= image_ends[:, None, :]).astype(jnp.int32), axis=2)
    row_alive = row_ids[None, :] < image_ends[:, -1:]
    image_index = jnp.minimum(image_index, images - 1).astype(jnp.int32)
    row_source = jnp.take_along_axis(source_ids, image_index, axis=1)
    row_weight = jnp.where(row_alive, loss_weights[row_source].astype(jnp.float32) * 0.25, jnp.float32(0.0))
    offset = (row_ids[None, :] - jnp.take_along_axis(image_starts, image_index, axis=1)).astype(jnp.int32)
    owners = jnp.where(row_alive, image_index, -1).astype(jnp.int32)
    weighted = (out_grad.reshape(groups, row_total, FEAT).astype(jnp.float32) * row_weight[:, :, None]).astype(jnp.bfloat16)
    grads = lax.map(block_step, (queries.reshape(groups, row_total, FEAT), keys.reshape(groups, row_total, FEAT),
                                 values.reshape(groups, row_total, FEAT), weighted, owners))
    pack_hits = pack_of[:, :, None] == jnp.arange(groups, dtype=jnp.int32)[None, None, :]
    incoming = jnp.sum(jnp.where(pack_hits, lengths[:, :, None], 0), axis=1).astype(jnp.int32)
    begins = (jnp.cumsum(incoming, axis=0) - incoming).astype(jnp.int32)
    image_ids = jnp.arange(images, dtype=jnp.int32)
    earlier = (pack_of[:, :, None] == pack_of[:, None, :]) & (image_ids[None, None, :] < image_ids[None, :, None])
    prior = jnp.sum(jnp.where(earlier, lengths[:, None, :], 0), axis=2).astype(jnp.int32)
    row_pack = jnp.take_along_axis(pack_of, image_index, axis=1).astype(jnp.int32)
    row_begin = jnp.take_along_axis(begins, row_pack, axis=1).astype(jnp.int32)
    row_prior = jnp.take_along_axis(prior, image_index, axis=1).astype(jnp.int32)
    pack_index = jnp.where(row_alive, row_pack * row_total + row_begin + row_prior + offset, groups * row_total)
    pack_index = pack_index.reshape(-1).astype(jnp.int32)

    def place(grad_block):
        empty = jnp.zeros((groups * row_total, FEAT), jnp.bfloat16)
        return empty.at[pack_index].set(grad_block.reshape(-1, FEAT), mode="drop")

    return place(grads[0]), place(grads[1]), place(grads[2])
```

```python
import jax
import jax.numpy as jnp
from jax import lax
from jax.experimental import pallas as pl
from jax.experimental.pallas import tpu as pltpu
from jax.sharding import PartitionSpec as P

HEAD_DIM = 128
PATCH_MAX = 8
MASKED = -1e30
SCALE = HEAD_DIM ** (-0.5)

NN = (((1,), (0,)), ((), ()))
NT = (((1,), (1,)), ((), ()))
TN = (((0,), (0,)), ((), ()))

STRIDE = 27
UNSTRIDE = 19

PARAMS = pltpu.CompilerParams(vmem_limit_bytes=48 * 1024 * 1024)


def dot(a, b, dims):
    return lax.dot_general(a, b, dims, preferred_element_type=jnp.float32)


def iota(shape, axis):
    return lax.broadcasted_iota(jnp.int32, shape, axis)


def low(mask):
    return mask.astype(jnp.float32).astype(jnp.bfloat16)


def split_kernel(q_ref, k_ref, v_ref, g_ref, out_ref, whole_ref, whole_sem, sem):
    ranks, _, width = out_ref.shape
    rows = q_ref.shape[0]
    whole_copies = [
        pltpu.make_async_copy(ref, whole_ref.at[at], whole_sem.at[at]) for at, ref in enumerate((q_ref, k_ref))
    ]
    copies = [
        pltpu.make_async_copy(
            ref.at[:, rank * width : (rank + 1) * width],
            out_ref.at[rank, at * rows : (at + 1) * rows, :],
            sem.at[at - 2, rank],
        )
        for at, ref in ((2, v_ref), (3, g_ref))
        for rank in range(ranks)
    ]
    for copy in whole_copies + copies:
        copy.start()
    for at, copy in enumerate(whole_copies):
        copy.wait()
        for rank in range(ranks):
            out_ref[rank, at * rows : (at + 1) * rows, :] = whole_ref[at, :, rank * width : (rank + 1) * width]
    for copy in copies:
        copy.wait()


def spread_column(column):
    return jnp.broadcast_to(column, (column.shape[0], 128)).astype(jnp.bfloat16)


def index_kernel(
    at_ref, lengths_ref, packs_ref, sources_ref, weights_ref, same_ref, scale_ref, out_place_ref, in_place_ref
):
    images, groups = lengths_ref.shape
    total = same_ref.shape[0]
    slots = groups * PATCH_MAX
    own = at_ref[0]

    lengths, packs = lengths_ref[...], packs_ref[...]
    mine = iota((images, groups), 1) == own
    lens = jnp.sum(jnp.where(mine, lengths, 0).astype(jnp.float32), axis=1, keepdims=True)
    pack = jnp.sum(jnp.where(mine, packs, 0).astype(jnp.float32), axis=1, keepdims=True)
    kind = jnp.sum(jnp.where(mine, sources_ref[...], 0).astype(jnp.float32), axis=1, keepdims=True)

    earlier = iota((images, images), 1) < iota((images, images), 0)
    lens_wide = spread_column(lens)
    starts = dot(low(earlier), lens_wide, NN)[:, 0:1]
    pack_hits = low(iota((images, groups), 1).astype(jnp.float32) == pack)
    same_pack = dot(pack_hits, pack_hits, NT) > 0.5
    prior = dot(low(same_pack & earlier), lens_wide, NN)[:, 0:1]

    row_id = iota((images, total), 1).astype(jnp.float32)
    offset = row_id - starts
    member = (offset >= 0) & (offset < lens)
    member_low = low(member)
    same_ref[...] = dot(member_low, member_low, TN).astype(jnp.bfloat16)

    weight = jnp.zeros((images, 1), jnp.float32)
    for at in range(weights_ref.shape[0]):
        weight = jnp.where(kind == at, weights_ref[at].astype(jnp.float32) * 0.25, weight)
    scale_ref[...] = dot(member_low, spread_column(weight), TN)

    place = pack * UNSTRIDE - jnp.floor(pack * (UNSTRIDE / groups)) * groups
    slot = jnp.sum(jnp.where(member, place * PATCH_MAX + prior + offset + 1.0, 0.0), axis=0, keepdims=True)
    slot = slot.astype(jnp.int32) - 1
    out_place_ref[...] = low(iota((slots, total), 0) == slot)

    arriving = jnp.where(packs == own, lengths, 0).astype(jnp.float32)
    incoming = jnp.broadcast_to(jnp.sum(arriving, axis=0, keepdims=True), (8, groups))
    before = low(iota((groups, groups), 0) < iota((groups, groups), 1))
    begins = dot(incoming.astype(jnp.bfloat16), before, NN)
    to_slots = low((iota((groups, slots), 1) // PATCH_MAX * STRIDE) % groups == iota((groups, slots), 0))
    begin_at = dot(begins.astype(jnp.bfloat16), to_slots, NN)[0:1]
    count_at = dot(incoming.astype(jnp.bfloat16), to_slots, NN)[0:1]
    within = (iota((1, slots), 1) % PATCH_MAX).astype(jnp.float32)
    row = jnp.where(within < count_at, begin_at + within, -1.0).astype(jnp.int32)
    in_place_ref[...] = low(iota((total, slots), 0) == row)


def grad_kernel(same_ref, scale_ref, place_ref, x_ref, out_ref):
    ranks, four_rows, width = x_ref.shape
    rows = four_rows // 4
    total = ranks * rows
    heads = range(width // HEAD_DIM)
    allowed = same_ref[...].astype(jnp.float32) > 0.5
    place = place_ref[...]

    def rows_of(at, head):
        cols = slice(head * HEAD_DIM, (head + 1) * HEAD_DIM)
        return x_ref[:, at * rows : (at + 1) * rows, cols].reshape(total, HEAD_DIM)

    def send(at, head, grad):
        to = at * width + head * HEAD_DIM
        out_ref[:, to : to + grad.shape[1]] = grad.astype(jnp.bfloat16)

    probs, dv = [], []
    for head in heads:
        scores = jnp.where(allowed, dot(rows_of(1, head), rows_of(0, head), NT) * SCALE, MASKED)
        exp_scores = jnp.exp(scores - jnp.max(scores, axis=0, keepdims=True))
        probs.append(exp_scores / jnp.sum(exp_scores, axis=0, keepdims=True))
    dk = []
    for head in heads:
        q, k, v = rows_of(0, head), rows_of(1, head), rows_of(2, head)
        g = (rows_of(3, head).astype(jnp.float32) * scale_ref[...]).astype(jnp.bfloat16)
        probs_low = probs[head].astype(jnp.bfloat16)
        dv.append(dot(probs_low, g, NN).astype(jnp.bfloat16))
        attn_out = dot(v, probs_low, TN)
        row_delta = jnp.sum(g.astype(jnp.float32).T * attn_out, axis=0, keepdims=True)
        grad_probs = dot(v, g, NT)
        grad_scores = (probs[head] * (grad_probs - row_delta)).astype(jnp.bfloat16)
        dk.append((dot(grad_scores, q, NN) * SCALE).astype(jnp.bfloat16))
        dq = (dot(k, grad_scores, TN) * SCALE).astype(jnp.bfloat16)
        send(0, head, dot(place, dq, NT))
    send(1, 0, dot(place, jnp.concatenate(dk, axis=1), NN))
    send(2, 0, dot(place, jnp.concatenate(dv, axis=1), NN))


def pack_kernel(place_ref, x_ref, out_ref):
    out_ref[...] = dot(place_ref[...], x_ref[...], NN).astype(jnp.bfloat16)


def join_kernel(x_ref, q_ref, k_ref, v_ref, whole_ref, sem):
    ranks, _, wide = x_ref.shape
    width = wide // 3
    copies = []
    for at, ref in enumerate((q_ref, k_ref, v_ref)):
        for rank in range(ranks):
            whole_ref[at, :, rank * width : (rank + 1) * width] = x_ref[rank, :, at * width : (at + 1) * width]
        copies.append(pltpu.make_async_copy(whole_ref.at[at], ref, sem.at[at]))
        copies[-1].start()
    for copy in copies:
        copy.wait()


def whole():
    return pl.BlockSpec(memory_space=pltpu.VMEM)


def scalars():
    return pl.BlockSpec(memory_space=pltpu.SMEM)


def in_place():
    return pl.BlockSpec(memory_space=pl.ANY)


def from_hbm(array):
    return pltpu.with_memory_space_constraint(array, pltpu.HBM)


def local(queries, keys, values, out_grad, lengths, pack_of, source_ids, loss_weights):
    groups = lax.axis_size("dp")
    ranks = lax.axis_size("tensor")
    index = lax.axis_index("dp").astype(jnp.int32).reshape(1)
    rows, feat = queries.shape
    width = feat // ranks
    total = rows * ranks
    slots = groups * PATCH_MAX
    bf16 = jnp.bfloat16

    by_rank = pl.pallas_call(
        split_kernel,
        out_shape=jax.ShapeDtypeStruct((ranks, 4 * rows, width), bf16),
        in_specs=[in_place()] * 4,
        out_specs=whole(),
        scratch_shapes=[
            pltpu.VMEM((2, rows, feat), bf16),
            pltpu.SemaphoreType.DMA((2,)),
            pltpu.SemaphoreType.DMA((2, ranks)),
        ],
        compiler_params=PARAMS,
    )(*(from_hbm(array) for array in (queries, keys, values, out_grad)))
    by_rank, index = lax.optimization_barrier((by_rank, index))
    by_head = lax.all_to_all(by_rank, "tensor", split_axis=0, concat_axis=0, tiled=True)
    same, scale, out_place, in_place_hot = pl.pallas_call(
        index_kernel,
        out_shape=(
            jax.ShapeDtypeStruct((total, total), bf16),
            jax.ShapeDtypeStruct((total, HEAD_DIM), jnp.float32),
            jax.ShapeDtypeStruct((slots, total), bf16),
            jax.ShapeDtypeStruct((total, slots), bf16),
        ),
        in_specs=[scalars(), whole(), whole(), whole(), scalars()],
        out_specs=(whole(),) * 4,
        compiler_params=PARAMS,
        cost_estimate=pl.CostEstimate(flops=1 << 24, bytes_accessed=1 << 20, transcendentals=0),
    )(index, from_hbm(lengths.T), from_hbm(pack_of.T), from_hbm(source_ids.T), loss_weights)
    in_slots = pl.pallas_call(
        grad_kernel,
        out_shape=jax.ShapeDtypeStruct((slots, 3 * width), bf16),
        in_specs=[whole()] * 4,
        out_specs=whole(),
        compiler_params=PARAMS,
    )(same, scale, out_place, by_head)
    arrived = lax.all_to_all(
        in_slots.reshape(groups, PATCH_MAX, 3 * width),
        "dp",
        split_axis=0,
        concat_axis=0,
        axis_index_groups=[[place * STRIDE % groups for place in range(groups)]],
        tiled=True,
    ).reshape(slots, 3 * width)
    packed = pl.pallas_call(
        pack_kernel,
        out_shape=jax.ShapeDtypeStruct((total, 3 * width), bf16),
        in_specs=[whole()] * 2,
        out_specs=whole(),
        compiler_params=PARAMS,
    )(in_place_hot, arrived)
    returned = lax.all_to_all(
        packed.reshape(ranks, rows, 3 * width), "tensor", split_axis=0, concat_axis=0, tiled=True
    )
    out = jax.ShapeDtypeStruct((rows, feat), bf16)
    return pl.pallas_call(
        join_kernel,
        out_shape=(out, out, out),
        in_specs=[whole()],
        out_specs=(in_place(), in_place(), in_place()),
        scratch_shapes=[pltpu.VMEM((3, rows, feat), bf16), pltpu.SemaphoreType.DMA((3,))],
        compiler_params=PARAMS,
    )(returned)


def solution(mesh):
    split = P(("dp", "tensor"), None)
    return jax.shard_map(
        local,
        mesh=mesh,
        in_specs=(split,) * 4 + (P(),) * 4,
        out_specs=(split,) * 3,
        check_vma=False,
    )
```

```python
import jax
import jax.numpy as jnp
from jax import lax
from jax.experimental import pallas as pl
from jax.experimental.pallas import tpu as pltpu
from jax.sharding import PartitionSpec as P

HEAD_DIM = 128
PATCH_MAX = 8
MASKED = -1e30
SCALE = HEAD_DIM ** (-0.5)

NN = (((1,), (0,)), ((), ()))
NT = (((1,), (1,)), ((), ()))
TN = (((0,), (0,)), ((), ()))

STRIDE = 27
UNSTRIDE = 19

PARAMS = pltpu.CompilerParams(vmem_limit_bytes=48 * 1024 * 1024)


def dot(a, b, dims):
    return lax.dot_general(a, b, dims, preferred_element_type=jnp.float32)


def iota(shape, axis):
    return lax.broadcasted_iota(jnp.int32, shape, axis)


def low(mask):
    return mask.astype(jnp.float32).astype(jnp.bfloat16)


def spread_column(column):
    return jnp.broadcast_to(column, (column.shape[0], 128)).astype(jnp.bfloat16)


def index_work(at_ref, lengths_ref, packs_ref, sources_ref, weights_ref, same_ref, scale_ref, out_place_ref, in_place_ref):
    images, groups = lengths_ref.shape
    total = same_ref.shape[0]
    slots = groups * PATCH_MAX
    own = at_ref[0]

    lengths, packs = lengths_ref[...], packs_ref[...]
    mine = iota((images, groups), 1) == own
    lens = jnp.sum(jnp.where(mine, lengths, 0).astype(jnp.float32), axis=1, keepdims=True)
    pack = jnp.sum(jnp.where(mine, packs, 0).astype(jnp.float32), axis=1, keepdims=True)
    kind = jnp.sum(jnp.where(mine, sources_ref[...], 0).astype(jnp.float32), axis=1, keepdims=True)

    earlier = iota((images, images), 1) < iota((images, images), 0)
    lens_wide = spread_column(lens)
    starts = dot(low(earlier), lens_wide, NN)[:, 0:1]
    pack_hits = low(iota((images, groups), 1).astype(jnp.float32) == pack)
    same_pack = dot(pack_hits, pack_hits, NT) > 0.5
    prior = dot(low(same_pack & earlier), lens_wide, NN)[:, 0:1]

    row_id = iota((images, total), 1).astype(jnp.float32)
    offset = row_id - starts
    member = (offset >= 0) & (offset < lens)
    member_low = low(member)
    same_ref[...] = dot(member_low, member_low, TN).astype(jnp.bfloat16)

    weight = jnp.zeros((images, 1), jnp.float32)
    for at in range(weights_ref.shape[0]):
        weight = jnp.where(kind == at, weights_ref[at].astype(jnp.float32) * 0.25, weight)
    scale_ref[...] = dot(member_low, spread_column(weight), TN)

    place = pack * UNSTRIDE - jnp.floor(pack * (UNSTRIDE / groups)) * groups
    slot = jnp.sum(jnp.where(member, place * PATCH_MAX + prior + offset + 1.0, 0.0), axis=0, keepdims=True)
    slot = slot.astype(jnp.int32) - 1
    out_place_ref[...] = low(iota((slots, total), 0) == slot)

    arriving = jnp.where(packs == own, lengths, 0).astype(jnp.float32)
    incoming = jnp.broadcast_to(jnp.sum(arriving, axis=0, keepdims=True), (8, groups))
    before = low(iota((groups, groups), 0) < iota((groups, groups), 1))
    begins = dot(incoming.astype(jnp.bfloat16), before, NN)
    to_slots = low((iota((groups, slots), 1) // PATCH_MAX * STRIDE) % groups == iota((groups, slots), 0))
    begin_at = dot(begins.astype(jnp.bfloat16), to_slots, NN)[0:1]
    count_at = dot(incoming.astype(jnp.bfloat16), to_slots, NN)[0:1]
    within = (iota((1, slots), 1) % PATCH_MAX).astype(jnp.float32)
    row = jnp.where(within < count_at, begin_at + within, -1.0).astype(jnp.int32)
    in_place_ref[...] = low(iota((total, slots), 0) == row)


def split_kernel(
    at_ref,
    weights_ref,
    lengths_hbm,
    packs_hbm,
    sources_hbm,
    q_ref,
    k_ref,
    v_ref,
    g_ref,
    out_ref,
    same_ref,
    scale_ref,
    out_place_ref,
    in_place_ref,
    number_ref,
    whole_ref,
    number_sem,
    whole_sem,
    sem,
):
    ranks, _, width = out_ref.shape
    rows = q_ref.shape[0]
    number_copies = [
        pltpu.make_async_copy(ref, number_ref.at[at], number_sem.at[at])
        for at, ref in enumerate((lengths_hbm, packs_hbm, sources_hbm))
    ]
    whole_copies = [
        pltpu.make_async_copy(ref, whole_ref.at[at], whole_sem.at[at]) for at, ref in enumerate((q_ref, k_ref))
    ]
    copies = [
        pltpu.make_async_copy(
            ref.at[:, rank * width : (rank + 1) * width],
            out_ref.at[rank, at * rows : (at + 1) * rows, :],
            sem.at[at - 2, rank],
        )
        for at, ref in ((2, v_ref), (3, g_ref))
        for rank in range(ranks)
    ]
    for copy in number_copies + whole_copies + copies:
        copy.start()
    for copy in number_copies:
        copy.wait()
    index_work(
        at_ref,
        number_ref.at[0],
        number_ref.at[1],
        number_ref.at[2],
        weights_ref,
        same_ref,
        scale_ref,
        out_place_ref,
        in_place_ref,
    )
    for at, copy in enumerate(whole_copies):
        copy.wait()
        for rank in range(ranks):
            out_ref[rank, at * rows : (at + 1) * rows, :] = whole_ref[at, :, rank * width : (rank + 1) * width]
    for copy in copies:
        copy.wait()


def grad_kernel(same_ref, scale_ref, place_ref, x_ref, out_ref):
    ranks, four_rows, width = x_ref.shape
    rows = four_rows // 4
    total = ranks * rows
    heads = range(width // HEAD_DIM)
    allowed = same_ref[...].astype(jnp.float32) > 0.5
    place = place_ref[...]

    def rows_of(at, head):
        cols = slice(head * HEAD_DIM, (head + 1) * HEAD_DIM)
        return x_ref[:, at * rows : (at + 1) * rows, cols].reshape(total, HEAD_DIM)

    def send(at, head, grad):
        to = at * width + head * HEAD_DIM
        out_ref[:, to : to + grad.shape[1]] = grad.astype(jnp.bfloat16)

    probs, dv = [], []
    for head in heads:
        scores = jnp.where(allowed, dot(rows_of(1, head), rows_of(0, head), NT) * SCALE, MASKED)
        exp_scores = jnp.exp(scores - jnp.max(scores, axis=0, keepdims=True))
        probs.append(exp_scores / jnp.sum(exp_scores, axis=0, keepdims=True))
    dk = []
    for head in heads:
        q, k, v = rows_of(0, head), rows_of(1, head), rows_of(2, head)
        g = (rows_of(3, head).astype(jnp.float32) * scale_ref[...]).astype(jnp.bfloat16)
        probs_low = probs[head].astype(jnp.bfloat16)
        dv.append(dot(probs_low, g, NN).astype(jnp.bfloat16))
        attn_out = dot(v, probs_low, TN)
        row_delta = jnp.sum(g.astype(jnp.float32).T * attn_out, axis=0, keepdims=True)
        grad_probs = dot(v, g, NT)
        grad_scores = (probs[head] * (grad_probs - row_delta)).astype(jnp.bfloat16)
        dk.append((dot(grad_scores, q, NN) * SCALE).astype(jnp.bfloat16))
        dq = (dot(k, grad_scores, TN) * SCALE).astype(jnp.bfloat16)
        send(0, head, dot(place, dq, NT))
    send(1, 0, dot(place, jnp.concatenate(dk, axis=1), NN))
    send(2, 0, dot(place, jnp.concatenate(dv, axis=1), NN))


def pack_kernel(place_ref, x_ref, out_ref):
    out_ref[...] = dot(place_ref[...], x_ref[...], NN).astype(jnp.bfloat16)


def join_kernel(x_ref, q_ref, k_ref, v_ref, whole_ref, sem):
    ranks, _, wide = x_ref.shape
    width = wide // 3
    copies = []
    for at, ref in enumerate((q_ref, k_ref, v_ref)):
        for rank in range(ranks):
            whole_ref[at, :, rank * width : (rank + 1) * width] = x_ref[rank, :, at * width : (at + 1) * width]
        copies.append(pltpu.make_async_copy(whole_ref.at[at], ref, sem.at[at]))
        copies[-1].start()
    for copy in copies:
        copy.wait()


def whole():
    return pl.BlockSpec(memory_space=pltpu.VMEM)


def scalars():
    return pl.BlockSpec(memory_space=pltpu.SMEM)


def in_place():
    return pl.BlockSpec(memory_space=pl.ANY)


def from_hbm(array):
    return pltpu.with_memory_space_constraint(array, pltpu.HBM)


def local(queries, keys, values, out_grad, lengths, pack_of, source_ids, loss_weights):
    groups = lax.axis_size("dp")
    ranks = lax.axis_size("tensor")
    index = lax.axis_index("dp").astype(jnp.int32).reshape(1)
    rows, feat = queries.shape
    width = feat // ranks
    total = rows * ranks
    slots = groups * PATCH_MAX
    bf16 = jnp.bfloat16

    numbers = (lengths.T, pack_of.T, source_ids.T)
    by_rank, same, scale, out_place, in_place_hot = pl.pallas_call(
        split_kernel,
        out_shape=(
            jax.ShapeDtypeStruct((ranks, 4 * rows, width), bf16),
            jax.ShapeDtypeStruct((total, total), bf16),
            jax.ShapeDtypeStruct((total, HEAD_DIM), jnp.float32),
            jax.ShapeDtypeStruct((slots, total), bf16),
            jax.ShapeDtypeStruct((total, slots), bf16),
        ),
        in_specs=[scalars(), scalars()] + [in_place()] * 7,
        out_specs=(whole(),) * 5,
        scratch_shapes=[
            pltpu.VMEM((3,) + numbers[0].shape, jnp.int32),
            pltpu.VMEM((2, rows, feat), bf16),
            pltpu.SemaphoreType.DMA((3,)),
            pltpu.SemaphoreType.DMA((2,)),
            pltpu.SemaphoreType.DMA((2, ranks)),
        ],
        compiler_params=PARAMS,
    )(index, *(from_hbm(array) for array in (loss_weights,) + numbers + (queries, keys, values, out_grad)))
    by_head = lax.all_to_all(by_rank, "tensor", split_axis=0, concat_axis=0, tiled=True)
    in_slots = pl.pallas_call(
        grad_kernel,
        out_shape=jax.ShapeDtypeStruct((slots, 3 * width), bf16),
        in_specs=[whole()] * 4,
        out_specs=whole(),
        compiler_params=PARAMS,
    )(same, scale, out_place, by_head)
    arrived = lax.all_to_all(
        in_slots.reshape(groups, PATCH_MAX, 3 * width),
        "dp",
        split_axis=0,
        concat_axis=0,
        axis_index_groups=[[place * STRIDE % groups for place in range(groups)]],
        tiled=True,
    ).reshape(slots, 3 * width)
    packed = pl.pallas_call(
        pack_kernel,
        out_shape=jax.ShapeDtypeStruct((total, 3 * width), bf16),
        in_specs=[whole()] * 2,
        out_specs=whole(),
        compiler_params=PARAMS,
    )(in_place_hot, arrived)
    returned = lax.all_to_all(
        packed.reshape(ranks, rows, 3 * width), "tensor", split_axis=0, concat_axis=0, tiled=True
    )
    out = jax.ShapeDtypeStruct((rows, feat), bf16)
    return pl.pallas_call(
        join_kernel,
        out_shape=(out, out, out),
        in_specs=[whole()],
        out_specs=(in_place(), in_place(), in_place()),
        scratch_shapes=[pltpu.VMEM((3, rows, feat), bf16), pltpu.SemaphoreType.DMA((3,))],
        compiler_params=PARAMS,
    )(returned)


def solution(mesh):
    split = P(("dp", "tensor"), None)
    return jax.shard_map(
        local,
        mesh=mesh,
        in_specs=(split,) * 4 + (P(),) * 4,
        out_specs=(split,) * 3,
        check_vma=False,
    )
```

```python
import jax
import jax.numpy as jnp
from jax import lax
from jax.experimental import pallas as pl
from jax.experimental.pallas import tpu as pltpu
from jax.sharding import PartitionSpec as P

HEAD_DIM = 128
PATCH_MAX = 8
MASKED = -1e30
SCALE = HEAD_DIM ** (-0.5)
SCALE_BASE2 = SCALE * 1.4426950408889634

NN = (((1,), (0,)), ((), ()))
NT = (((1,), (1,)), ((), ()))
TN = (((0,), (0,)), ((), ()))

STRIDE = 27
UNSTRIDE = 19

PARAMS = pltpu.CompilerParams(vmem_limit_bytes=48 * 1024 * 1024)


def dot(a, b, dims):
    return lax.dot_general(a, b, dims, preferred_element_type=jnp.float32)


def iota(shape, axis):
    return lax.broadcasted_iota(jnp.int32, shape, axis)


def low(mask):
    return mask.astype(jnp.float32).astype(jnp.bfloat16)


def split_kernel(q_ref, k_ref, v_ref, g_ref, out_ref, whole_ref, built_ref, whole_sem, sem, out_sem):
    ranks, _, width = out_ref.shape
    rows = q_ref.shape[0]
    whole_copies = [
        pltpu.make_async_copy(ref, whole_ref.at[at], whole_sem.at[at]) for at, ref in enumerate((q_ref, k_ref))
    ]
    copies = [
        pltpu.make_async_copy(
            ref.at[:, rank * width : (rank + 1) * width],
            built_ref.at[rank, at * rows : (at + 1) * rows, :],
            sem.at[at - 2, rank],
        )
        for at, ref in ((2, v_ref), (3, g_ref))
        for rank in range(ranks)
    ]
    for copy in whole_copies + copies:
        copy.start()
    for at, copy in enumerate(whole_copies):
        copy.wait()
        for rank in range(ranks):
            built_ref[rank, at * rows : (at + 1) * rows, :] = whole_ref[at, :, rank * width : (rank + 1) * width]
    halves = [
        pltpu.make_async_copy(
            built_ref.at[:, half * rows : (half + 2) * rows, :],
            out_ref.at[:, half * rows : (half + 2) * rows, :],
            out_sem.at[half // 2],
        )
        for half in (0, 2)
    ]
    halves[0].start()
    for copy in copies:
        copy.wait()
    halves[1].start()
    for copy in halves:
        copy.wait()


def spread_column(column):
    return jnp.broadcast_to(column, (column.shape[0], 128)).astype(jnp.bfloat16)


def index_kernel(
    at_ref, lengths_ref, packs_ref, sources_ref, weights_ref, same_ref, scale_ref, out_place_ref, in_place_ref
):
    images, groups = lengths_ref.shape
    total = same_ref.shape[0]
    slots = groups * PATCH_MAX
    own = at_ref[0]

    lengths, packs = lengths_ref[...], packs_ref[...]
    mine = iota((images, groups), 1) == own
    lens = jnp.sum(jnp.where(mine, lengths, 0).astype(jnp.float32), axis=1, keepdims=True)
    pack = jnp.sum(jnp.where(mine, packs, 0).astype(jnp.float32), axis=1, keepdims=True)
    kind = jnp.sum(jnp.where(mine, sources_ref[...], 0).astype(jnp.float32), axis=1, keepdims=True)

    earlier = iota((images, images), 1) < iota((images, images), 0)
    lens_wide = spread_column(lens)
    starts = dot(low(earlier), lens_wide, NN)[:, 0:1]
    pack_hits = low(iota((images, groups), 1).astype(jnp.float32) == pack)
    same_pack = dot(pack_hits, pack_hits, NT) > 0.5
    prior = dot(low(same_pack & earlier), lens_wide, NN)[:, 0:1]

    row_id = iota((images, total), 1).astype(jnp.float32)
    offset = row_id - starts
    member = (offset >= 0) & (offset < lens)
    member_low = low(member)
    same_ref[...] = jnp.where(dot(member_low, member_low, TN) > 0.5, 0.0, MASKED)

    weight = jnp.zeros((images, 1), jnp.float32)
    for at in range(weights_ref.shape[0]):
        weight = jnp.where(kind == at, weights_ref[at].astype(jnp.float32) * 0.25, weight)
    scale_ref[...] = dot(member_low, spread_column(weight), TN)

    place = pack * UNSTRIDE - jnp.floor(pack * (UNSTRIDE / groups)) * groups
    slot = jnp.sum(jnp.where(member, place * PATCH_MAX + prior + offset + 1.0, 0.0), axis=0, keepdims=True)
    slot = slot.astype(jnp.int32) - 1
    out_place_ref[...] = low(iota((slots, total), 0) == slot)

    arriving = jnp.where(packs == own, lengths, 0).astype(jnp.float32)
    incoming = jnp.broadcast_to(jnp.sum(arriving, axis=0, keepdims=True), (8, groups))
    before = low(iota((groups, groups), 0) < iota((groups, groups), 1))
    begins = dot(incoming.astype(jnp.bfloat16), before, NN)
    to_slots = low((iota((groups, slots), 1) // PATCH_MAX * STRIDE) % groups == iota((groups, slots), 0))
    begin_at = dot(begins.astype(jnp.bfloat16), to_slots, NN)[0:1]
    count_at = dot(incoming.astype(jnp.bfloat16), to_slots, NN)[0:1]
    within = (iota((1, slots), 1) % PATCH_MAX).astype(jnp.float32)
    row = jnp.where(within < count_at, begin_at + within, -1.0).astype(jnp.int32)
    in_place_ref[...] = low(iota((total, slots), 0) == row)


def grad_kernel(same_ref, scale_ref, place_ref, x_ref, out_ref):
    ranks, four_rows, width = x_ref.shape
    rows = four_rows // 4
    total = ranks * rows
    heads = range(width // HEAD_DIM)
    mask = same_ref[...]
    place = place_ref[...]

    def rows_of(at, head):
        cols = slice(head * HEAD_DIM, (head + 1) * HEAD_DIM)
        return x_ref[:, at * rows : (at + 1) * rows, cols].reshape(total, HEAD_DIM)

    def send(at, product):
        out_ref[:, at * width : (at + 1) * width] = product.astype(jnp.bfloat16)

    probs, grad_probs, dv = [], [], []
    for head in heads:
        scores = dot(rows_of(1, head), rows_of(0, head), NT) * SCALE_BASE2 + mask
        exp_scores = jnp.exp2(scores - jnp.max(scores, axis=0, keepdims=True))
        probs.append(exp_scores * (1.0 / jnp.sum(exp_scores, axis=0, keepdims=True)))
        g = (rows_of(3, head).astype(jnp.float32) * scale_ref[...]).astype(jnp.bfloat16)
        grad_probs.append(dot(rows_of(2, head), g, NT))
        dv.append(dot(probs[head].astype(jnp.bfloat16), g, NN).astype(jnp.bfloat16))
    dq, dk = [], []
    for head in heads:
        probs_low = probs[head].astype(jnp.bfloat16).astype(jnp.float32)
        row_delta = jnp.sum(probs_low * grad_probs[head], axis=0, keepdims=True)
        grad_scores = (probs[head] * (grad_probs[head] - row_delta)).astype(jnp.bfloat16)
        dk.append((dot(grad_scores, rows_of(0, head), NN) * SCALE).astype(jnp.bfloat16))
        dq.append((dot(rows_of(1, head), grad_scores, TN) * SCALE).astype(jnp.bfloat16))
    send(2, dot(place, jnp.concatenate(dv, axis=1), NN))
    send(1, dot(place, jnp.concatenate(dk, axis=1), NN))
    send(0, dot(place, jnp.concatenate(dq, axis=0), NT))


def pack_kernel(place_ref, x_ref, out_ref):
    out_ref[...] = dot(place_ref[...], x_ref[...], NN).astype(jnp.bfloat16)


def join_kernel(x_ref, q_ref, k_ref, v_ref, whole_ref, sem):
    ranks, _, wide = x_ref.shape
    width = wide // 3
    copies = []
    for at, ref in enumerate((q_ref, k_ref, v_ref)):
        for rank in range(ranks):
            whole_ref[at, :, rank * width : (rank + 1) * width] = x_ref[rank, :, at * width : (at + 1) * width]
        copies.append(pltpu.make_async_copy(whole_ref.at[at], ref, sem.at[at]))
        copies[-1].start()
    for copy in copies:
        copy.wait()


def whole():
    return pl.BlockSpec(memory_space=pltpu.VMEM)


def scalars():
    return pl.BlockSpec(memory_space=pltpu.SMEM)


def in_place():
    return pl.BlockSpec(memory_space=pl.ANY)


def from_hbm(array):
    return pltpu.with_memory_space_constraint(array, pltpu.HBM)


def local(queries, keys, values, out_grad, lengths, pack_of, source_ids, loss_weights):
    groups = lax.axis_size("dp")
    ranks = lax.axis_size("tensor")
    index = lax.axis_index("dp").astype(jnp.int32).reshape(1)
    rows, feat = queries.shape
    width = feat // ranks
    total = rows * ranks
    slots = groups * PATCH_MAX
    bf16 = jnp.bfloat16

    by_rank = pl.pallas_call(
        split_kernel,
        out_shape=jax.ShapeDtypeStruct((ranks, 4 * rows, width), bf16),
        in_specs=[in_place()] * 4,
        out_specs=in_place(),
        scratch_shapes=[
            pltpu.VMEM((2, rows, feat), bf16),
            pltpu.VMEM((ranks, 4 * rows, width), bf16),
            pltpu.SemaphoreType.DMA((2,)),
            pltpu.SemaphoreType.DMA((2, ranks)),
            pltpu.SemaphoreType.DMA((2,)),
        ],
        compiler_params=PARAMS,
    )(*(from_hbm(array) for array in (queries, keys, values, out_grad)))
    by_rank, index = lax.optimization_barrier((by_rank, index))
    by_head = lax.all_to_all(by_rank, "tensor", split_axis=0, concat_axis=0, tiled=True)
    same, scale, out_place, in_place_hot = pl.pallas_call(
        index_kernel,
        out_shape=(
            jax.ShapeDtypeStruct((total, total), jnp.float32),
            jax.ShapeDtypeStruct((total, HEAD_DIM), jnp.float32),
            jax.ShapeDtypeStruct((slots, total), bf16),
            jax.ShapeDtypeStruct((total, slots), bf16),
        ),
        in_specs=[scalars(), whole(), whole(), whole(), scalars()],
        out_specs=(whole(),) * 4,
        compiler_params=PARAMS,
        cost_estimate=pl.CostEstimate(flops=1 << 24, bytes_accessed=1 << 20, transcendentals=0),
    )(index, from_hbm(lengths.T), from_hbm(pack_of.T), from_hbm(source_ids.T), loss_weights)
    in_slots = pl.pallas_call(
        grad_kernel,
        out_shape=jax.ShapeDtypeStruct((slots, 3 * width), bf16),
        in_specs=[whole()] * 4,
        out_specs=whole(),
        compiler_params=PARAMS,
    )(same, scale, out_place, by_head)
    arrived = lax.all_to_all(
        in_slots.reshape(groups, PATCH_MAX, 3 * width),
        "dp",
        split_axis=0,
        concat_axis=0,
        axis_index_groups=[[place * STRIDE % groups for place in range(groups)]],
        tiled=True,
    ).reshape(slots, 3 * width)
    packed = pl.pallas_call(
        pack_kernel,
        out_shape=jax.ShapeDtypeStruct((total, 3 * width), bf16),
        in_specs=[whole()] * 2,
        out_specs=whole(),
        compiler_params=PARAMS,
    )(in_place_hot, arrived)
    returned = lax.all_to_all(
        packed.reshape(ranks, rows, 3 * width), "tensor", split_axis=0, concat_axis=0, tiled=True
    )
    out = jax.ShapeDtypeStruct((rows, feat), bf16)
    return pl.pallas_call(
        join_kernel,
        out_shape=(out, out, out),
        in_specs=[whole()],
        out_specs=(in_place(), in_place(), in_place()),
        scratch_shapes=[pltpu.VMEM((3, rows, feat), bf16), pltpu.SemaphoreType.DMA((3,))],
        compiler_params=PARAMS,
    )(returned)


def solution(mesh):
    split = P(("dp", "tensor"), None)
    return jax.shard_map(
        local,
        mesh=mesh,
        in_specs=(split,) * 4 + (P(),) * 4,
        out_specs=(split,) * 3,
        check_vma=False,
    )
```

```python
import jax
import jax.numpy as jnp
from jax import lax
from jax.experimental import pallas as pl
from jax.experimental.pallas import tpu as pltpu
from jax.sharding import PartitionSpec as P

HEAD_DIM = 128
PATCH_MAX = 8
MASKED = -1e30
SCALE = HEAD_DIM ** (-0.5)
SCALE_BASE2 = SCALE * 1.4426950408889634

NN = (((1,), (0,)), ((), ()))
NT = (((1,), (1,)), ((), ()))
TN = (((0,), (0,)), ((), ()))

STRIDE = 27
UNSTRIDE = 19

PARAMS = pltpu.CompilerParams(vmem_limit_bytes=48 * 1024 * 1024)


def dot(a, b, dims):
    return lax.dot_general(a, b, dims, preferred_element_type=jnp.float32)


def iota(shape, axis):
    return lax.broadcasted_iota(jnp.int32, shape, axis)


def low(mask):
    return mask.astype(jnp.float32).astype(jnp.bfloat16)


def split_kernel(q_ref, k_ref, v_ref, g_ref, out_ref, whole_ref, whole_sem, sem):
    ranks, _, width = out_ref.shape
    rows = q_ref.shape[0]
    whole_copies = [
        pltpu.make_async_copy(ref, whole_ref.at[at], whole_sem.at[at]) for at, ref in enumerate((q_ref, k_ref))
    ]
    copies = [
        pltpu.make_async_copy(
            ref.at[:, rank * width : (rank + 1) * width],
            out_ref.at[rank, at * rows : (at + 1) * rows, :],
            sem.at[at - 2, rank],
        )
        for at, ref in ((2, v_ref), (3, g_ref))
        for rank in range(ranks)
    ]
    for copy in whole_copies + copies:
        copy.start()
    for at, copy in enumerate(whole_copies):
        copy.wait()
        for rank in range(ranks):
            out_ref[rank, at * rows : (at + 1) * rows, :] = whole_ref[at, :, rank * width : (rank + 1) * width]
    for copy in copies:
        copy.wait()


def spread_column(column):
    return jnp.broadcast_to(column, (column.shape[0], 128)).astype(jnp.bfloat16)


def index_kernel(
    at_ref, lengths_ref, packs_ref, sources_ref, weights_ref, same_ref, scale_ref, out_place_ref, in_place_ref
):
    images, groups = lengths_ref.shape
    total = same_ref.shape[0]
    slots = groups * PATCH_MAX
    own = at_ref[0]

    lengths, packs = lengths_ref[...], packs_ref[...]
    mine = iota((images, groups), 1) == own
    lens = jnp.sum(jnp.where(mine, lengths, 0).astype(jnp.float32), axis=1, keepdims=True)
    pack = jnp.sum(jnp.where(mine, packs, 0).astype(jnp.float32), axis=1, keepdims=True)
    kind = jnp.sum(jnp.where(mine, sources_ref[...], 0).astype(jnp.float32), axis=1, keepdims=True)

    earlier = iota((images, images), 1) < iota((images, images), 0)
    lens_wide = spread_column(lens)
    starts = dot(low(earlier), lens_wide, NN)[:, 0:1]
    pack_hits = low(iota((images, groups), 1).astype(jnp.float32) == pack)
    same_pack = dot(pack_hits, pack_hits, NT) > 0.5
    prior = dot(low(same_pack & earlier), lens_wide, NN)[:, 0:1]

    row_id = iota((images, total), 1).astype(jnp.float32)
    offset = row_id - starts
    member = (offset >= 0) & (offset < lens)
    member_low = low(member)
    same_ref[...] = jnp.where(dot(member_low, member_low, TN) > 0.5, 0.0, MASKED)

    weight = jnp.zeros((images, 1), jnp.float32)
    for at in range(weights_ref.shape[0]):
        weight = jnp.where(kind == at, weights_ref[at].astype(jnp.float32) * 0.25, weight)
    scale_ref[...] = dot(member_low, spread_column(weight), TN)

    place = pack * UNSTRIDE - jnp.floor(pack * (UNSTRIDE / groups)) * groups
    slot = jnp.sum(jnp.where(member, place * PATCH_MAX + prior + offset + 1.0, 0.0), axis=0, keepdims=True)
    slot = slot.astype(jnp.int32) - 1
    out_place_ref[...] = low(iota((slots, total), 0) == slot)

    arriving = jnp.where(packs == own, lengths, 0).astype(jnp.float32)
    incoming = jnp.broadcast_to(jnp.sum(arriving, axis=0, keepdims=True), (8, groups))
    before = low(iota((groups, groups), 0) < iota((groups, groups), 1))
    begins = dot(incoming.astype(jnp.bfloat16), before, NN)
    to_slots = low((iota((groups, slots), 1) // PATCH_MAX * STRIDE) % groups == iota((groups, slots), 0))
    begin_at = dot(begins.astype(jnp.bfloat16), to_slots, NN)[0:1]
    count_at = dot(incoming.astype(jnp.bfloat16), to_slots, NN)[0:1]
    within = (iota((1, slots), 1) % PATCH_MAX).astype(jnp.float32)
    row = jnp.where(within < count_at, begin_at + within, -1.0).astype(jnp.int32)
    in_place_ref[...] = low(iota((total, slots), 0) == row)


def grad_kernel(same_ref, scale_ref, place_ref, x_ref, out_ref):
    ranks, four_rows, width = x_ref.shape
    rows = four_rows // 4
    total = ranks * rows
    heads = range(width // HEAD_DIM)
    mask = same_ref[...]
    place = place_ref[...]

    def rows_of(at, head):
        cols = slice(head * HEAD_DIM, (head + 1) * HEAD_DIM)
        return x_ref[:, at * rows : (at + 1) * rows, cols].reshape(total, HEAD_DIM)

    def send(at, product):
        out_ref[:, at * width : (at + 1) * width] = product.astype(jnp.bfloat16)

    probs, grad_probs, dv = [], [], []
    for head in heads:
        scores = dot(rows_of(1, head), rows_of(0, head), NT) * SCALE_BASE2 + mask
        exp_scores = jnp.exp2(scores - jnp.max(scores, axis=0, keepdims=True))
        probs.append(exp_scores * (1.0 / jnp.sum(exp_scores, axis=0, keepdims=True)))
        g = (rows_of(3, head).astype(jnp.float32) * scale_ref[...]).astype(jnp.bfloat16)
        grad_probs.append(dot(rows_of(2, head), g, NT))
        dv.append(dot(probs[head].astype(jnp.bfloat16), g, NN).astype(jnp.bfloat16))
    dq, dk = [], []
    for head in heads:
        probs_low = probs[head].astype(jnp.bfloat16).astype(jnp.float32)
        row_delta = jnp.sum(probs_low * grad_probs[head], axis=0, keepdims=True)
        grad_scores = (probs[head] * (grad_probs[head] - row_delta)).astype(jnp.bfloat16)
        dk.append((dot(grad_scores, rows_of(0, head), NN) * SCALE).astype(jnp.bfloat16))
        dq.append((dot(rows_of(1, head), grad_scores, TN) * SCALE).astype(jnp.bfloat16))
    send(2, dot(place, jnp.concatenate(dv, axis=1), NN))
    send(1, dot(place, jnp.concatenate(dk, axis=1), NN))
    send(0, dot(place, jnp.concatenate(dq, axis=0), NT))


def pack_kernel(place_ref, x_ref, out_ref):
    out_ref[...] = dot(place_ref[...], x_ref[...], NN).astype(jnp.bfloat16)


def join_kernel(x_ref, q_ref, k_ref, v_ref, whole_ref, sem):
    ranks, _, wide = x_ref.shape
    width = wide // 3
    copies = []
    for at, ref in enumerate((q_ref, k_ref, v_ref)):
        for rank in range(ranks):
            whole_ref[at, :, rank * width : (rank + 1) * width] = x_ref[rank, :, at * width : (at + 1) * width]
        copies.append(pltpu.make_async_copy(whole_ref.at[at], ref, sem.at[at]))
        copies[-1].start()
    for copy in copies:
        copy.wait()


def whole():
    return pl.BlockSpec(memory_space=pltpu.VMEM)


def scalars():
    return pl.BlockSpec(memory_space=pltpu.SMEM)


def in_place():
    return pl.BlockSpec(memory_space=pl.ANY)


def from_hbm(array):
    return pltpu.with_memory_space_constraint(array, pltpu.HBM)


def local(queries, keys, values, out_grad, lengths, pack_of, source_ids, loss_weights):
    groups = lax.axis_size("dp")
    ranks = lax.axis_size("tensor")
    index = lax.axis_index("dp").astype(jnp.int32).reshape(1)
    rows, feat = queries.shape
    width = feat // ranks
    total = rows * ranks
    slots = groups * PATCH_MAX
    bf16 = jnp.bfloat16

    by_rank = pl.pallas_call(
        split_kernel,
        out_shape=pltpu.VMEM((ranks, 4 * rows, width), bf16),
        in_specs=[in_place()] * 4,
        out_specs=whole(),
        scratch_shapes=[
            pltpu.VMEM((2, rows, feat), bf16),
            pltpu.SemaphoreType.DMA((2,)),
            pltpu.SemaphoreType.DMA((2, ranks)),
        ],
        compiler_params=PARAMS,
    )(*(from_hbm(array) for array in (queries, keys, values, out_grad)))
    by_rank, index = lax.optimization_barrier((by_rank, index))
    by_head = lax.all_to_all(by_rank, "tensor", split_axis=0, concat_axis=0, tiled=True)
    same, scale, out_place, in_place_hot = pl.pallas_call(
        index_kernel,
        out_shape=(
            jax.ShapeDtypeStruct((total, total), jnp.float32),
            jax.ShapeDtypeStruct((total, HEAD_DIM), jnp.float32),
            jax.ShapeDtypeStruct((slots, total), bf16),
            jax.ShapeDtypeStruct((total, slots), bf16),
        ),
        in_specs=[scalars(), whole(), whole(), whole(), scalars()],
        out_specs=(whole(),) * 4,
        compiler_params=PARAMS,
        cost_estimate=pl.CostEstimate(flops=1 << 24, bytes_accessed=1 << 20, transcendentals=0),
    )(index, from_hbm(lengths.T), from_hbm(pack_of.T), from_hbm(source_ids.T), loss_weights)
    in_slots = pl.pallas_call(
        grad_kernel,
        out_shape=jax.ShapeDtypeStruct((slots, 3 * width), bf16),
        in_specs=[whole()] * 4,
        out_specs=whole(),
        compiler_params=PARAMS,
    )(same, scale, out_place, by_head)
    arrived = lax.all_to_all(
        in_slots.reshape(groups, PATCH_MAX, 3 * width),
        "dp",
        split_axis=0,
        concat_axis=0,
        axis_index_groups=[[place * STRIDE % groups for place in range(groups)]],
        tiled=True,
    ).reshape(slots, 3 * width)
    packed = pl.pallas_call(
        pack_kernel,
        out_shape=jax.ShapeDtypeStruct((total, 3 * width), bf16),
        in_specs=[whole()] * 2,
        out_specs=whole(),
        compiler_params=PARAMS,
    )(in_place_hot, arrived)
    returned = lax.all_to_all(
        packed.reshape(ranks, rows, 3 * width), "tensor", split_axis=0, concat_axis=0, tiled=True
    )
    out = jax.ShapeDtypeStruct((rows, feat), bf16)
    return pl.pallas_call(
        join_kernel,
        out_shape=(out, out, out),
        in_specs=[whole()],
        out_specs=(in_place(), in_place(), in_place()),
        scratch_shapes=[pltpu.VMEM((3, rows, feat), bf16), pltpu.SemaphoreType.DMA((3,))],
        compiler_params=PARAMS,
    )(returned)


def solution(mesh):
    split = P(("dp", "tensor"), None)
    return jax.shard_map(
        local,
        mesh=mesh,
        in_specs=(split,) * 4 + (P(),) * 4,
        out_specs=(split,) * 3,
        check_vma=False,
    )
```

```python
import jax
import jax.numpy as jnp
from jax import lax
from jax.experimental import pallas as pl
from jax.experimental.pallas import tpu as pltpu
from jax.sharding import PartitionSpec as P

HEAD_DIM = 128
PATCH_MAX = 8
MASKED = -1e30
SCALE = HEAD_DIM ** (-0.5)
SCALE_BASE2 = SCALE * 1.4426950408889634

NN = (((1,), (0,)), ((), ()))
NT = (((1,), (1,)), ((), ()))
TN = (((0,), (0,)), ((), ()))

STRIDE = 27
UNSTRIDE = 19

PARAMS = pltpu.CompilerParams(vmem_limit_bytes=48 * 1024 * 1024)


def dot(a, b, dims):
    return lax.dot_general(a, b, dims, preferred_element_type=jnp.float32)


def iota(shape, axis):
    return lax.broadcasted_iota(jnp.int32, shape, axis)


def low(mask):
    return mask.astype(jnp.float32).astype(jnp.bfloat16)


def split_kernel(q_ref, k_ref, v_ref, g_ref, out_ref, whole_ref, sem):
    ranks = out_ref.shape[0]
    rows, feat = q_ref.shape
    heads = feat // HEAD_DIM // ranks
    copies = [
        pltpu.make_async_copy(ref, whole_ref.at[at], sem.at[at]) for at, ref in enumerate((q_ref, k_ref, v_ref, g_ref))
    ]
    for copy in copies:
        copy.start()
    for at, copy in enumerate(copies):
        copy.wait()
        for rank in range(ranks):
            for head in range(heads):
                to = (head * 4 + at) * rows
                col = (rank * heads + head) * HEAD_DIM
                out_ref[rank, to : to + rows, :] = whole_ref[at, :, col : col + HEAD_DIM]


def spread_column(column):
    return jnp.broadcast_to(column, (column.shape[0], 128)).astype(jnp.bfloat16)


def index_kernel(
    at_ref, lengths_ref, packs_ref, sources_ref, weights_ref, same_ref, scale_ref, out_place_ref, in_place_ref
):
    images, groups = lengths_ref.shape
    total = same_ref.shape[0]
    slots = groups * PATCH_MAX
    own = at_ref[0]

    lengths, packs = lengths_ref[...], packs_ref[...]
    mine = iota((images, groups), 1) == own
    lens = jnp.sum(jnp.where(mine, lengths, 0).astype(jnp.float32), axis=1, keepdims=True)
    pack = jnp.sum(jnp.where(mine, packs, 0).astype(jnp.float32), axis=1, keepdims=True)
    kind = jnp.sum(jnp.where(mine, sources_ref[...], 0).astype(jnp.float32), axis=1, keepdims=True)

    earlier = iota((images, images), 1) < iota((images, images), 0)
    lens_wide = spread_column(lens)
    starts = dot(low(earlier), lens_wide, NN)[:, 0:1]
    pack_hits = low(iota((images, groups), 1).astype(jnp.float32) == pack)
    same_pack = dot(pack_hits, pack_hits, NT) > 0.5
    prior = dot(low(same_pack & earlier), lens_wide, NN)[:, 0:1]

    row_id = iota((images, total), 1).astype(jnp.float32)
    offset = row_id - starts
    member = (offset >= 0) & (offset < lens)
    member_low = low(member)
    same_ref[...] = jnp.where(dot(member_low, member_low, TN) > 0.5, 0.0, MASKED)

    weight = jnp.zeros((images, 1), jnp.float32)
    for at in range(weights_ref.shape[0]):
        weight = jnp.where(kind == at, weights_ref[at].astype(jnp.float32) * 0.25, weight)
    scale_ref[...] = dot(member_low, spread_column(weight), TN)

    place = pack * UNSTRIDE - jnp.floor(pack * (UNSTRIDE / groups)) * groups
    slot = jnp.sum(jnp.where(member, place * PATCH_MAX + prior + offset + 1.0, 0.0), axis=0, keepdims=True)
    slot = slot.astype(jnp.int32) - 1
    out_place_ref[...] = low(iota((slots, total), 0) == slot)

    arriving = jnp.where(packs == own, lengths, 0).astype(jnp.float32)
    incoming = jnp.broadcast_to(jnp.sum(arriving, axis=0, keepdims=True), (8, groups))
    before = low(iota((groups, groups), 0) < iota((groups, groups), 1))
    begins = dot(incoming.astype(jnp.bfloat16), before, NN)
    to_slots = low((iota((groups, slots), 1) // PATCH_MAX * STRIDE) % groups == iota((groups, slots), 0))
    begin_at = dot(begins.astype(jnp.bfloat16), to_slots, NN)[0:1]
    count_at = dot(incoming.astype(jnp.bfloat16), to_slots, NN)[0:1]
    within = (iota((1, slots), 1) % PATCH_MAX).astype(jnp.float32)
    row = jnp.where(within < count_at, begin_at + within, -1.0).astype(jnp.int32)
    in_place_ref[...] = low(iota((total, slots), 0) == row)


def grad_kernel(same_ref, scale_ref, place_ref, x_ref, out_ref):
    ranks = x_ref.shape[0]
    total = same_ref.shape[0]
    rows = total // ranks
    width = out_ref.shape[1] // 3
    heads = range(width // HEAD_DIM)
    mask = same_ref[...]
    place = place_ref[...]

    def rows_of(at, head):
        begin = (head * 4 + at) * rows
        return x_ref[:, begin : begin + rows, :].reshape(total, HEAD_DIM)

    def send(at, product):
        out_ref[:, at * width : (at + 1) * width] = product.astype(jnp.bfloat16)

    probs, grad_probs, dv = [], [], []
    for head in heads:
        scores = dot(rows_of(1, head), rows_of(0, head), NT) * SCALE_BASE2 + mask
        exp_scores = jnp.exp2(scores - jnp.max(scores, axis=0, keepdims=True))
        probs.append(exp_scores * (1.0 / jnp.sum(exp_scores, axis=0, keepdims=True)))
        g = (rows_of(3, head).astype(jnp.float32) * scale_ref[...]).astype(jnp.bfloat16)
        grad_probs.append(dot(rows_of(2, head), g, NT))
        dv.append(dot(probs[head].astype(jnp.bfloat16), g, NN).astype(jnp.bfloat16))
    dq, dk = [], []
    for head in heads:
        probs_low = probs[head].astype(jnp.bfloat16).astype(jnp.float32)
        row_delta = jnp.sum(probs_low * grad_probs[head], axis=0, keepdims=True)
        grad_scores = (probs[head] * (grad_probs[head] - row_delta)).astype(jnp.bfloat16)
        dk.append((dot(grad_scores, rows_of(0, head), NN) * SCALE).astype(jnp.bfloat16))
        dq.append((dot(rows_of(1, head), grad_scores, TN) * SCALE).astype(jnp.bfloat16))
    send(2, dot(place, jnp.concatenate(dv, axis=1), NN))
    send(1, dot(place, jnp.concatenate(dk, axis=1), NN))
    send(0, dot(place, jnp.concatenate(dq, axis=0), NT))


def pack_kernel(place_ref, x_ref, out_ref):
    ranks, three_rows, width = out_ref.shape
    rows = three_rows // 3
    packed = dot(place_ref[...], x_ref[...], NN).astype(jnp.bfloat16)
    for rank in range(ranks):
        for at in range(3):
            out_ref[rank, at * rows : (at + 1) * rows, :] = packed[
                rank * rows : (rank + 1) * rows, at * width : (at + 1) * width
            ]


def join_kernel(x_ref, q_ref, k_ref, v_ref, whole_ref, sem):
    ranks, three_rows, width = x_ref.shape
    rows = three_rows // 3
    copies = []
    for at, ref in enumerate((q_ref, k_ref, v_ref)):
        for rank in range(ranks):
            whole_ref[at, :, rank * width : (rank + 1) * width] = x_ref[rank, at * rows : (at + 1) * rows, :]
        copies.append(pltpu.make_async_copy(whole_ref.at[at], ref, sem.at[at]))
        copies[-1].start()
    for copy in copies:
        copy.wait()


def whole():
    return pl.BlockSpec(memory_space=pltpu.VMEM)


def scalars():
    return pl.BlockSpec(memory_space=pltpu.SMEM)


def in_place():
    return pl.BlockSpec(memory_space=pl.ANY)


def from_hbm(array):
    return pltpu.with_memory_space_constraint(array, pltpu.HBM)


def local(queries, keys, values, out_grad, lengths, pack_of, source_ids, loss_weights):
    groups = lax.axis_size("dp")
    ranks = lax.axis_size("tensor")
    index = lax.axis_index("dp").astype(jnp.int32).reshape(1)
    rows, feat = queries.shape
    width = feat // ranks
    total = rows * ranks
    slots = groups * PATCH_MAX
    bf16 = jnp.bfloat16

    by_rank = pl.pallas_call(
        split_kernel,
        out_shape=jax.ShapeDtypeStruct((ranks, 4 * rows * (width // HEAD_DIM), HEAD_DIM), bf16),
        in_specs=[in_place()] * 4,
        out_specs=whole(),
        scratch_shapes=[pltpu.VMEM((4, rows, feat), bf16), pltpu.SemaphoreType.DMA((4,))],
        compiler_params=PARAMS,
    )(*(from_hbm(array) for array in (queries, keys, values, out_grad)))
    by_rank, index = lax.optimization_barrier((by_rank, index))
    by_head = lax.all_to_all(by_rank, "tensor", split_axis=0, concat_axis=0, tiled=True)
    same, scale, out_place, in_place_hot = pl.pallas_call(
        index_kernel,
        out_shape=(
            jax.ShapeDtypeStruct((total, total), jnp.float32),
            jax.ShapeDtypeStruct((total, HEAD_DIM), jnp.float32),
            jax.ShapeDtypeStruct((slots, total), bf16),
            jax.ShapeDtypeStruct((total, slots), bf16),
        ),
        in_specs=[scalars(), whole(), whole(), whole(), scalars()],
        out_specs=(whole(),) * 4,
        compiler_params=PARAMS,
        cost_estimate=pl.CostEstimate(flops=1 << 24, bytes_accessed=1 << 20, transcendentals=0),
    )(index, from_hbm(lengths.T), from_hbm(pack_of.T), from_hbm(source_ids.T), loss_weights)
    in_slots = pl.pallas_call(
        grad_kernel,
        out_shape=jax.ShapeDtypeStruct((slots, 3 * width), bf16),
        in_specs=[whole()] * 4,
        out_specs=whole(),
        compiler_params=PARAMS,
    )(same, scale, out_place, by_head)
    arrived = lax.all_to_all(
        in_slots.reshape(groups, PATCH_MAX, 3 * width),
        "dp",
        split_axis=0,
        concat_axis=0,
        axis_index_groups=[[place * STRIDE % groups for place in range(groups)]],
        tiled=True,
    ).reshape(slots, 3 * width)
    packed = pl.pallas_call(
        pack_kernel,
        out_shape=jax.ShapeDtypeStruct((ranks, 3 * rows, width), bf16),
        in_specs=[whole()] * 2,
        out_specs=whole(),
        compiler_params=PARAMS,
    )(in_place_hot, arrived)
    returned = lax.all_to_all(packed, "tensor", split_axis=0, concat_axis=0, tiled=True)
    out = jax.ShapeDtypeStruct((rows, feat), bf16)
    return pl.pallas_call(
        join_kernel,
        out_shape=(out, out, out),
        in_specs=[whole()],
        out_specs=(in_place(), in_place(), in_place()),
        scratch_shapes=[pltpu.VMEM((3, rows, feat), bf16), pltpu.SemaphoreType.DMA((3,))],
        compiler_params=PARAMS,
    )(returned)


def solution(mesh):
    split = P(("dp", "tensor"), None)
    return jax.shard_map(
        local,
        mesh=mesh,
        in_specs=(split,) * 4 + (P(),) * 4,
        out_specs=(split,) * 3,
        check_vma=False,
    )
```

```python
import jax
import jax.numpy as jnp
from jax import lax
from jax.experimental import pallas as pl
from jax.experimental.pallas import tpu as pltpu
from jax.sharding import PartitionSpec as P

HEAD_DIM = 128
PATCH_MAX = 8
MASKED = -1e30
SCALE = HEAD_DIM ** (-0.5)
SCALE_BASE2 = SCALE * 1.4426950408889634

NN = (((1,), (0,)), ((), ()))
NT = (((1,), (1,)), ((), ()))
TN = (((0,), (0,)), ((), ()))

STRIDE = 27
UNSTRIDE = 19

PARAMS = pltpu.CompilerParams(vmem_limit_bytes=48 * 1024 * 1024)


def dot(a, b, dims):
    return lax.dot_general(a, b, dims, preferred_element_type=jnp.float32)


def iota(shape, axis):
    return lax.broadcasted_iota(jnp.int32, shape, axis)


def low(mask):
    return mask.astype(jnp.float32).astype(jnp.bfloat16)


def split_kernel(q_ref, k_ref, v_ref, g_ref, out_ref, whole_ref, built_ref, sem, out_sem):
    ranks = out_ref.shape[0]
    rows, feat = q_ref.shape
    heads = feat // HEAD_DIM // ranks
    half = rows // 2
    copies = [
        pltpu.make_async_copy(
            ref.at[part * half : (part + 1) * half, :],
            whole_ref.at[at, part * half : (part + 1) * half, :],
            sem.at[at, part],
        )
        for at, ref in enumerate((q_ref, k_ref, v_ref, g_ref))
        for part in range(2)
    ]
    for copy in copies:
        copy.start()
    for copy in copies:
        copy.wait()
    sends = []
    for rank in range(ranks):
        for head in range(heads):
            for at in range(4):
                to = (head * 4 + at) * rows
                col = (rank * heads + head) * HEAD_DIM
                built_ref[rank, to : to + rows, :] = whole_ref[at, :, col : col + HEAD_DIM]
        sends.append(pltpu.make_async_copy(built_ref.at[rank], out_ref.at[rank], out_sem.at[rank]))
        sends[-1].start()
    for send in sends:
        send.wait()


def spread_column(column):
    return jnp.broadcast_to(column, (column.shape[0], 128)).astype(jnp.bfloat16)


def index_kernel(
    at_ref, lengths_ref, packs_ref, sources_ref, weights_ref, same_ref, scale_ref, out_place_ref, in_place_ref
):
    images, groups = lengths_ref.shape
    total = same_ref.shape[0]
    slots = groups * PATCH_MAX
    own = at_ref[0]

    lengths, packs = lengths_ref[...], packs_ref[...]
    mine = iota((images, groups), 1) == own
    lens = jnp.sum(jnp.where(mine, lengths, 0).astype(jnp.float32), axis=1, keepdims=True)
    pack = jnp.sum(jnp.where(mine, packs, 0).astype(jnp.float32), axis=1, keepdims=True)
    kind = jnp.sum(jnp.where(mine, sources_ref[...], 0).astype(jnp.float32), axis=1, keepdims=True)

    earlier = iota((images, images), 1) < iota((images, images), 0)
    lens_wide = spread_column(lens)
    starts = dot(low(earlier), lens_wide, NN)[:, 0:1]
    pack_hits = low(iota((images, groups), 1).astype(jnp.float32) == pack)
    same_pack = dot(pack_hits, pack_hits, NT) > 0.5
    prior = dot(low(same_pack & earlier), lens_wide, NN)[:, 0:1]

    row_id = iota((images, total), 1).astype(jnp.float32)
    offset = row_id - starts
    member = (offset >= 0) & (offset < lens)
    member_low = low(member)
    same_ref[...] = jnp.where(dot(member_low, member_low, TN) > 0.5, 0.0, MASKED)

    weight = jnp.zeros((images, 1), jnp.float32)
    for at in range(weights_ref.shape[0]):
        weight = jnp.where(kind == at, weights_ref[at].astype(jnp.float32) * 0.25, weight)
    scale_ref[...] = dot(member_low, spread_column(weight), TN)

    place = pack * UNSTRIDE - jnp.floor(pack * (UNSTRIDE / groups)) * groups
    slot = jnp.sum(jnp.where(member, place * PATCH_MAX + prior + offset + 1.0, 0.0), axis=0, keepdims=True)
    slot = slot.astype(jnp.int32) - 1
    out_place_ref[...] = low(iota((slots, total), 0) == slot)

    arriving = jnp.where(packs == own, lengths, 0).astype(jnp.float32)
    incoming = jnp.broadcast_to(jnp.sum(arriving, axis=0, keepdims=True), (8, groups))
    before = low(iota((groups, groups), 0) < iota((groups, groups), 1))
    begins = dot(incoming.astype(jnp.bfloat16), before, NN)
    to_slots = low((iota((groups, slots), 1) // PATCH_MAX * STRIDE) % groups == iota((groups, slots), 0))
    begin_at = dot(begins.astype(jnp.bfloat16), to_slots, NN)[0:1]
    count_at = dot(incoming.astype(jnp.bfloat16), to_slots, NN)[0:1]
    within = (iota((1, slots), 1) % PATCH_MAX).astype(jnp.float32)
    row = jnp.where(within < count_at, begin_at + within, -1.0).astype(jnp.int32)
    in_place_ref[...] = low(iota((total, slots), 0) == row)


def grad_kernel(same_ref, scale_ref, place_ref, x_ref, out_ref):
    ranks = x_ref.shape[0]
    total = same_ref.shape[0]
    rows = total // ranks
    width = out_ref.shape[1] // 3
    heads = range(width // HEAD_DIM)
    mask = same_ref[...]
    place = place_ref[...]

    def rows_of(at, head):
        begin = (head * 4 + at) * rows
        return x_ref[:, begin : begin + rows, :].reshape(total, HEAD_DIM)

    def send(at, product):
        out_ref[:, at * width : (at + 1) * width] = product.astype(jnp.bfloat16)

    probs, grad_probs, dv = [], [], []
    for head in heads:
        scores = dot(rows_of(1, head), rows_of(0, head), NT) * SCALE_BASE2 + mask
        exp_scores = jnp.exp2(scores - jnp.max(scores, axis=0, keepdims=True))
        probs.append(exp_scores * (1.0 / jnp.sum(exp_scores, axis=0, keepdims=True)))
        g = (rows_of(3, head).astype(jnp.float32) * scale_ref[...]).astype(jnp.bfloat16)
        grad_probs.append(dot(rows_of(2, head), g, NT))
        dv.append(dot(probs[head].astype(jnp.bfloat16), g, NN).astype(jnp.bfloat16))
    dq, dk = [], []
    for head in heads:
        probs_low = probs[head].astype(jnp.bfloat16).astype(jnp.float32)
        row_delta = jnp.sum(probs_low * grad_probs[head], axis=0, keepdims=True)
        grad_scores = (probs[head] * (grad_probs[head] - row_delta)).astype(jnp.bfloat16)
        dk.append((dot(grad_scores, rows_of(0, head), NN) * SCALE).astype(jnp.bfloat16))
        dq.append((dot(rows_of(1, head), grad_scores, TN) * SCALE).astype(jnp.bfloat16))
    send(2, dot(place, jnp.concatenate(dv, axis=1), NN))
    send(1, dot(place, jnp.concatenate(dk, axis=1), NN))
    send(0, dot(place, jnp.concatenate(dq, axis=0), NT))


def pack_kernel(place_ref, x_ref, out_ref):
    ranks, three_rows, width = out_ref.shape
    rows = three_rows // 3
    packed = dot(place_ref[...], x_ref[...], NN).astype(jnp.bfloat16)
    for rank in range(ranks):
        for at in range(3):
            out_ref[rank, at * rows : (at + 1) * rows, :] = packed[
                rank * rows : (rank + 1) * rows, at * width : (at + 1) * width
            ]


def join_kernel(x_ref, q_ref, k_ref, v_ref, whole_ref, sem):
    ranks, three_rows, width = x_ref.shape
    rows = three_rows // 3
    half = rows // 2
    copies = []
    for at, ref in enumerate((q_ref, k_ref, v_ref)):
        for part in range(2):
            here = slice(part * half, (part + 1) * half)
            begin = at * rows + part * half
            for rank in range(ranks):
                whole_ref[at, here, rank * width : (rank + 1) * width] = x_ref[rank, begin : begin + half, :]
            copies.append(pltpu.make_async_copy(whole_ref.at[at, here, :], ref.at[here, :], sem.at[at, part]))
            copies[-1].start()
    for copy in copies:
        copy.wait()


def whole():
    return pl.BlockSpec(memory_space=pltpu.VMEM)


def scalars():
    return pl.BlockSpec(memory_space=pltpu.SMEM)


def in_place():
    return pl.BlockSpec(memory_space=pl.ANY)


def from_hbm(array):
    return pltpu.with_memory_space_constraint(array, pltpu.HBM)


def local(queries, keys, values, out_grad, lengths, pack_of, source_ids, loss_weights):
    groups = lax.axis_size("dp")
    ranks = lax.axis_size("tensor")
    index = lax.axis_index("dp").astype(jnp.int32).reshape(1)
    rows, feat = queries.shape
    width = feat // ranks
    total = rows * ranks
    slots = groups * PATCH_MAX
    bf16 = jnp.bfloat16

    by_rank = pl.pallas_call(
        split_kernel,
        out_shape=jax.ShapeDtypeStruct((ranks, 4 * rows * (width // HEAD_DIM), HEAD_DIM), bf16),
        in_specs=[in_place()] * 4,
        out_specs=in_place(),
        scratch_shapes=[
            pltpu.VMEM((4, rows, feat), bf16),
            pltpu.VMEM((ranks, 4 * rows * (width // HEAD_DIM), HEAD_DIM), bf16),
            pltpu.SemaphoreType.DMA((4, 2)),
            pltpu.SemaphoreType.DMA((ranks,)),
        ],
        compiler_params=PARAMS,
    )(*(from_hbm(array) for array in (queries, keys, values, out_grad)))
    by_rank, index = lax.optimization_barrier((by_rank, index))
    by_head = lax.all_to_all(by_rank, "tensor", split_axis=0, concat_axis=0, tiled=True)
    same, scale, out_place, in_place_hot = pl.pallas_call(
        index_kernel,
        out_shape=(
            jax.ShapeDtypeStruct((total, total), jnp.float32),
            jax.ShapeDtypeStruct((total, HEAD_DIM), jnp.float32),
            jax.ShapeDtypeStruct((slots, total), bf16),
            jax.ShapeDtypeStruct((total, slots), bf16),
        ),
        in_specs=[scalars(), whole(), whole(), whole(), scalars()],
        out_specs=(whole(),) * 4,
        compiler_params=PARAMS,
        cost_estimate=pl.CostEstimate(flops=1 << 24, bytes_accessed=1 << 20, transcendentals=0),
    )(index, from_hbm(lengths.T), from_hbm(pack_of.T), from_hbm(source_ids.T), loss_weights)
    in_slots = pl.pallas_call(
        grad_kernel,
        out_shape=jax.ShapeDtypeStruct((slots, 3 * width), bf16),
        in_specs=[whole()] * 4,
        out_specs=whole(),
        compiler_params=PARAMS,
    )(same, scale, out_place, by_head)
    arrived = lax.all_to_all(
        in_slots.reshape(groups, PATCH_MAX, 3 * width),
        "dp",
        split_axis=0,
        concat_axis=0,
        axis_index_groups=[[place * STRIDE % groups for place in range(groups)]],
        tiled=True,
    ).reshape(slots, 3 * width)
    packed = pl.pallas_call(
        pack_kernel,
        out_shape=jax.ShapeDtypeStruct((ranks, 3 * rows, width), bf16),
        in_specs=[whole()] * 2,
        out_specs=whole(),
        compiler_params=PARAMS,
    )(in_place_hot, arrived)
    returned = lax.all_to_all(packed, "tensor", split_axis=0, concat_axis=0, tiled=True)
    out = jax.ShapeDtypeStruct((rows, feat), bf16)
    return pl.pallas_call(
        join_kernel,
        out_shape=(out, out, out),
        in_specs=[whole()],
        out_specs=(in_place(), in_place(), in_place()),
        scratch_shapes=[pltpu.VMEM((3, rows, feat), bf16), pltpu.SemaphoreType.DMA((3, 2))],
        compiler_params=PARAMS,
    )(returned)


def solution(mesh):
    split = P(("dp", "tensor"), None)
    return jax.shard_map(
        local,
        mesh=mesh,
        in_specs=(split,) * 4 + (P(),) * 4,
        out_specs=(split,) * 3,
        check_vma=False,
    )
```

```python
import jax
import jax.numpy as jnp
from jax import lax
from jax.experimental import pallas as pl
from jax.experimental.pallas import tpu as pltpu
from jax.sharding import PartitionSpec as P

HEAD_DIM = 128
PATCH_MAX = 8
MASKED = -1e30
SCALE = HEAD_DIM ** (-0.5)
SCALE_BASE2 = SCALE * 1.4426950408889634

NN = (((1,), (0,)), ((), ()))
NT = (((1,), (1,)), ((), ()))
TN = (((0,), (0,)), ((), ()))

STRIDE = 45
UNSTRIDE = 37

PARAMS = pltpu.CompilerParams(vmem_limit_bytes=48 * 1024 * 1024)


def dot(a, b, dims):
    return lax.dot_general(a, b, dims, preferred_element_type=jnp.float32)


def iota(shape, axis):
    return lax.broadcasted_iota(jnp.int32, shape, axis)


def low(mask):
    return mask.astype(jnp.float32).astype(jnp.bfloat16)


def split_kernel(q_ref, k_ref, v_ref, g_ref, out_ref, whole_ref, sem):
    ranks = out_ref.shape[0]
    rows, feat = q_ref.shape
    heads = feat // HEAD_DIM // ranks
    copies = [
        pltpu.make_async_copy(ref, whole_ref.at[at], sem.at[at]) for at, ref in enumerate((q_ref, k_ref, v_ref, g_ref))
    ]
    for copy in copies:
        copy.start()
    for at, copy in enumerate(copies):
        copy.wait()
        for rank in range(ranks):
            for head in range(heads):
                to = (head * 4 + at) * rows
                col = (rank * heads + head) * HEAD_DIM
                out_ref[rank, to : to + rows, :] = whole_ref[at, :, col : col + HEAD_DIM]


def spread_column(column):
    return jnp.broadcast_to(column, (column.shape[0], 128)).astype(jnp.bfloat16)


def index_kernel(
    at_ref, lengths_ref, packs_ref, sources_ref, weights_ref, same_ref, scale_ref, out_place_ref, in_place_ref
):
    images, groups = lengths_ref.shape
    total = same_ref.shape[0]
    slots = groups * PATCH_MAX
    own = at_ref[0]

    lengths, packs = lengths_ref[...], packs_ref[...]
    mine = iota((images, groups), 1) == own
    lens = jnp.sum(jnp.where(mine, lengths, 0).astype(jnp.float32), axis=1, keepdims=True)
    pack = jnp.sum(jnp.where(mine, packs, 0).astype(jnp.float32), axis=1, keepdims=True)
    kind = jnp.sum(jnp.where(mine, sources_ref[...], 0).astype(jnp.float32), axis=1, keepdims=True)

    earlier = iota((images, images), 1) < iota((images, images), 0)
    lens_wide = spread_column(lens)
    starts = dot(low(earlier), lens_wide, NN)[:, 0:1]
    pack_hits = low(iota((images, groups), 1).astype(jnp.float32) == pack)
    same_pack = dot(pack_hits, pack_hits, NT) > 0.5
    prior = dot(low(same_pack & earlier), lens_wide, NN)[:, 0:1]

    row_id = iota((images, total), 1).astype(jnp.float32)
    offset = row_id - starts
    member = (offset >= 0) & (offset < lens)
    member_low = low(member)
    same_ref[...] = jnp.where(dot(member_low, member_low, TN) > 0.5, 0.0, MASKED)

    weight = jnp.zeros((images, 1), jnp.float32)
    for at in range(weights_ref.shape[0]):
        weight = jnp.where(kind == at, weights_ref[at].astype(jnp.float32) * 0.25, weight)
    scale_ref[...] = dot(member_low, spread_column(weight), TN)

    place = pack * UNSTRIDE - jnp.floor(pack * (UNSTRIDE / groups)) * groups
    slot = jnp.sum(jnp.where(member, place * PATCH_MAX + prior + offset + 1.0, 0.0), axis=0, keepdims=True)
    slot = slot.astype(jnp.int32) - 1
    out_place_ref[...] = low(iota((slots, total), 0) == slot)

    arriving = jnp.where(packs == own, lengths, 0).astype(jnp.float32)
    incoming = jnp.broadcast_to(jnp.sum(arriving, axis=0, keepdims=True), (8, groups))
    before = low(iota((groups, groups), 0) < iota((groups, groups), 1))
    begins = dot(incoming.astype(jnp.bfloat16), before, NN)
    to_slots = low((iota((groups, slots), 1) // PATCH_MAX * STRIDE) % groups == iota((groups, slots), 0))
    begin_at = dot(begins.astype(jnp.bfloat16), to_slots, NN)[0:1]
    count_at = dot(incoming.astype(jnp.bfloat16), to_slots, NN)[0:1]
    within = (iota((1, slots), 1) % PATCH_MAX).astype(jnp.float32)
    row = jnp.where(within < count_at, begin_at + within, -1.0).astype(jnp.int32)
    in_place_ref[...] = low(iota((total, slots), 0) == row)


def grad_kernel(same_ref, scale_ref, place_ref, x_ref, out_ref):
    ranks = x_ref.shape[0]
    total = same_ref.shape[0]
    rows = total // ranks
    width = out_ref.shape[1] // 3
    heads = range(width // HEAD_DIM)
    mask = same_ref[...]
    place = place_ref[...]

    def rows_of(at, head):
        begin = (head * 4 + at) * rows
        return x_ref[:, begin : begin + rows, :].reshape(total, HEAD_DIM)

    def send(at, product):
        out_ref[:, at * width : (at + 1) * width] = product.astype(jnp.bfloat16)

    probs, grad_probs, dv = [], [], []
    for head in heads:
        scores = dot(rows_of(1, head), rows_of(0, head), NT) * SCALE_BASE2 + mask
        exp_scores = jnp.exp2(scores - jnp.max(scores, axis=0, keepdims=True))
        probs.append(exp_scores * (1.0 / jnp.sum(exp_scores, axis=0, keepdims=True)))
        g = (rows_of(3, head).astype(jnp.float32) * scale_ref[...]).astype(jnp.bfloat16)
        grad_probs.append(dot(rows_of(2, head), g, NT))
        dv.append(dot(probs[head].astype(jnp.bfloat16), g, NN).astype(jnp.bfloat16))
    dq, dk = [], []
    for head in heads:
        probs_low = probs[head].astype(jnp.bfloat16).astype(jnp.float32)
        row_delta = jnp.sum(probs_low * grad_probs[head], axis=0, keepdims=True)
        grad_scores = (probs[head] * (grad_probs[head] - row_delta)).astype(jnp.bfloat16)
        dk.append((dot(grad_scores, rows_of(0, head), NN) * SCALE).astype(jnp.bfloat16))
        dq.append((dot(rows_of(1, head), grad_scores, TN) * SCALE).astype(jnp.bfloat16))
    send(2, dot(place, jnp.concatenate(dv, axis=1), NN))
    send(1, dot(place, jnp.concatenate(dk, axis=1), NN))
    send(0, dot(place, jnp.concatenate(dq, axis=0), NT))


def pack_kernel(place_ref, x_ref, out_ref):
    ranks, three_rows, width = out_ref.shape
    rows = three_rows // 3
    packed = dot(place_ref[...], x_ref[...], NN).astype(jnp.bfloat16)
    for rank in range(ranks):
        for at in range(3):
            out_ref[rank, at * rows : (at + 1) * rows, :] = packed[
                rank * rows : (rank + 1) * rows, at * width : (at + 1) * width
            ]


def join_kernel(x_ref, q_ref, k_ref, v_ref, whole_ref, sem):
    ranks, three_rows, width = x_ref.shape
    rows = three_rows // 3
    copies = []
    for at, ref in enumerate((q_ref, k_ref, v_ref)):
        for rank in range(ranks):
            whole_ref[at, :, rank * width : (rank + 1) * width] = x_ref[rank, at * rows : (at + 1) * rows, :]
        copies.append(pltpu.make_async_copy(whole_ref.at[at], ref, sem.at[at]))
        copies[-1].start()
    for copy in copies:
        copy.wait()


def whole():
    return pl.BlockSpec(memory_space=pltpu.VMEM)


def scalars():
    return pl.BlockSpec(memory_space=pltpu.SMEM)


def in_place():
    return pl.BlockSpec(memory_space=pl.ANY)


def from_hbm(array):
    return pltpu.with_memory_space_constraint(array, pltpu.HBM)


def local(queries, keys, values, out_grad, lengths, pack_of, source_ids, loss_weights):
    groups = lax.axis_size("dp")
    ranks = lax.axis_size("tensor")
    index = lax.axis_index("dp").astype(jnp.int32).reshape(1)
    rows, feat = queries.shape
    width = feat // ranks
    total = rows * ranks
    slots = groups * PATCH_MAX
    bf16 = jnp.bfloat16

    by_rank = pl.pallas_call(
        split_kernel,
        out_shape=jax.ShapeDtypeStruct((ranks, 4 * rows * (width // HEAD_DIM), HEAD_DIM), bf16),
        in_specs=[in_place()] * 4,
        out_specs=whole(),
        scratch_shapes=[pltpu.VMEM((4, rows, feat), bf16), pltpu.SemaphoreType.DMA((4,))],
        compiler_params=PARAMS,
    )(*(from_hbm(array) for array in (queries, keys, values, out_grad)))
    by_rank, index = lax.optimization_barrier((by_rank, index))
    by_head = lax.all_to_all(by_rank, "tensor", split_axis=0, concat_axis=0, tiled=True)
    same, scale, out_place, in_place_hot = pl.pallas_call(
        index_kernel,
        out_shape=(
            jax.ShapeDtypeStruct((total, total), jnp.float32),
            jax.ShapeDtypeStruct((total, HEAD_DIM), jnp.float32),
            jax.ShapeDtypeStruct((slots, total), bf16),
            jax.ShapeDtypeStruct((total, slots), bf16),
        ),
        in_specs=[scalars(), whole(), whole(), whole(), scalars()],
        out_specs=(whole(),) * 4,
        compiler_params=PARAMS,
        cost_estimate=pl.CostEstimate(flops=1 << 24, bytes_accessed=1 << 20, transcendentals=0),
    )(index, from_hbm(lengths.T), from_hbm(pack_of.T), from_hbm(source_ids.T), loss_weights)
    in_slots = pl.pallas_call(
        grad_kernel,
        out_shape=jax.ShapeDtypeStruct((slots, 3 * width), bf16),
        in_specs=[whole()] * 4,
        out_specs=whole(),
        compiler_params=PARAMS,
    )(same, scale, out_place, by_head)
    arrived = lax.all_to_all(
        in_slots.reshape(groups, PATCH_MAX, 3 * width),
        "dp",
        split_axis=0,
        concat_axis=0,
        axis_index_groups=[[place * STRIDE % groups for place in range(groups)]],
        tiled=True,
    ).reshape(slots, 3 * width)
    packed = pl.pallas_call(
        pack_kernel,
        out_shape=jax.ShapeDtypeStruct((ranks, 3 * rows, width), bf16),
        in_specs=[whole()] * 2,
        out_specs=whole(),
        compiler_params=PARAMS,
    )(in_place_hot, arrived)
    returned = lax.all_to_all(packed, "tensor", split_axis=0, concat_axis=0, tiled=True)
    out = jax.ShapeDtypeStruct((rows, feat), bf16)
    return pl.pallas_call(
        join_kernel,
        out_shape=(out, out, out),
        in_specs=[whole()],
        out_specs=(in_place(), in_place(), in_place()),
        scratch_shapes=[pltpu.VMEM((3, rows, feat), bf16), pltpu.SemaphoreType.DMA((3,))],
        compiler_params=PARAMS,
    )(returned)


def solution(mesh):
    split = P(("dp", "tensor"), None)
    return jax.shard_map(
        local,
        mesh=mesh,
        in_specs=(split,) * 4 + (P(),) * 4,
        out_specs=(split,) * 3,
        check_vma=False,
    )
```

```python
import jax
import jax.numpy as jnp
from jax import lax
from jax.experimental import pallas as pl
from jax.experimental.pallas import tpu as pltpu
from jax.sharding import PartitionSpec as P

HEAD_DIM = 128
PATCH_MAX = 8
MASKED = -1e30
SCALE = HEAD_DIM ** (-0.5)
SCALE_BASE2 = SCALE * 1.4426950408889634

NN = (((1,), (0,)), ((), ()))
NT = (((1,), (1,)), ((), ()))
TN = (((0,), (0,)), ((), ()))

STRIDE = 29
UNSTRIDE = 53

PARAMS = pltpu.CompilerParams(vmem_limit_bytes=48 * 1024 * 1024)


def dot(a, b, dims):
    return lax.dot_general(a, b, dims, preferred_element_type=jnp.float32)


def iota(shape, axis):
    return lax.broadcasted_iota(jnp.int32, shape, axis)


def low(mask):
    return mask.astype(jnp.float32).astype(jnp.bfloat16)


def split_kernel(q_ref, k_ref, v_ref, g_ref, out_ref, whole_ref, sem):
    ranks = out_ref.shape[0]
    rows, feat = q_ref.shape
    heads = feat // HEAD_DIM // ranks
    copies = [
        pltpu.make_async_copy(ref, whole_ref.at[at], sem.at[at]) for at, ref in enumerate((q_ref, k_ref, v_ref, g_ref))
    ]
    for copy in copies:
        copy.start()
    for at, copy in enumerate(copies):
        copy.wait()
        for rank in range(ranks):
            for head in range(heads):
                to = (head * 4 + at) * rows
                col = (rank * heads + head) * HEAD_DIM
                out_ref[rank, to : to + rows, :] = whole_ref[at, :, col : col + HEAD_DIM]


def spread_column(column):
    return jnp.broadcast_to(column, (column.shape[0], 128)).astype(jnp.bfloat16)


def index_kernel(
    at_ref, lengths_ref, packs_ref, sources_ref, weights_ref, same_ref, scale_ref, out_place_ref, in_place_ref
):
    images, groups = lengths_ref.shape
    total = same_ref.shape[0]
    slots = groups * PATCH_MAX
    own = at_ref[0]

    lengths, packs = lengths_ref[...], packs_ref[...]
    mine = iota((images, groups), 1) == own
    lens = jnp.sum(jnp.where(mine, lengths, 0).astype(jnp.float32), axis=1, keepdims=True)
    pack = jnp.sum(jnp.where(mine, packs, 0).astype(jnp.float32), axis=1, keepdims=True)
    kind = jnp.sum(jnp.where(mine, sources_ref[...], 0).astype(jnp.float32), axis=1, keepdims=True)

    earlier = iota((images, images), 1) < iota((images, images), 0)
    lens_wide = spread_column(lens)
    starts = dot(low(earlier), lens_wide, NN)[:, 0:1]
    pack_hits = low(iota((images, groups), 1).astype(jnp.float32) == pack)
    same_pack = dot(pack_hits, pack_hits, NT) > 0.5
    prior = dot(low(same_pack & earlier), lens_wide, NN)[:, 0:1]

    row_id = iota((images, total), 1).astype(jnp.float32)
    offset = row_id - starts
    member = (offset >= 0) & (offset < lens)
    member_low = low(member)
    same_ref[...] = jnp.where(dot(member_low, member_low, TN) > 0.5, 0.0, MASKED)

    weight = jnp.zeros((images, 1), jnp.float32)
    for at in range(weights_ref.shape[0]):
        weight = jnp.where(kind == at, weights_ref[at].astype(jnp.float32) * 0.25, weight)
    scale_ref[...] = dot(member_low, spread_column(weight), TN)

    place = pack * UNSTRIDE - jnp.floor(pack * (UNSTRIDE / groups)) * groups
    slot = jnp.sum(jnp.where(member, place * PATCH_MAX + prior + offset + 1.0, 0.0), axis=0, keepdims=True)
    slot = slot.astype(jnp.int32) - 1
    out_place_ref[...] = low(iota((slots, total), 0) == slot)

    arriving = jnp.where(packs == own, lengths, 0).astype(jnp.float32)
    incoming = jnp.broadcast_to(jnp.sum(arriving, axis=0, keepdims=True), (8, groups))
    before = low(iota((groups, groups), 0) < iota((groups, groups), 1))
    begins = dot(incoming.astype(jnp.bfloat16), before, NN)
    to_slots = low((iota((groups, slots), 1) // PATCH_MAX * STRIDE) % groups == iota((groups, slots), 0))
    begin_at = dot(begins.astype(jnp.bfloat16), to_slots, NN)[0:1]
    count_at = dot(incoming.astype(jnp.bfloat16), to_slots, NN)[0:1]
    within = (iota((1, slots), 1) % PATCH_MAX).astype(jnp.float32)
    row = jnp.where(within < count_at, begin_at + within, -1.0).astype(jnp.int32)
    in_place_ref[...] = low(iota((total, slots), 0) == row)


def grad_kernel(same_ref, scale_ref, place_ref, x_ref, out_ref):
    ranks = x_ref.shape[0]
    total = same_ref.shape[0]
    rows = total // ranks
    width = out_ref.shape[1] // 3
    heads = range(width // HEAD_DIM)
    mask = same_ref[...]
    place = place_ref[...]

    def rows_of(at, head):
        begin = (head * 4 + at) * rows
        return x_ref[:, begin : begin + rows, :].reshape(total, HEAD_DIM)

    def send(at, product):
        out_ref[:, at * width : (at + 1) * width] = product.astype(jnp.bfloat16)

    probs, grad_probs, dv = [], [], []
    for head in heads:
        scores = dot(rows_of(1, head), rows_of(0, head), NT) * SCALE_BASE2 + mask
        exp_scores = jnp.exp2(scores - jnp.max(scores, axis=0, keepdims=True))
        probs.append(exp_scores * (1.0 / jnp.sum(exp_scores, axis=0, keepdims=True)))
        g = (rows_of(3, head).astype(jnp.float32) * scale_ref[...]).astype(jnp.bfloat16)
        grad_probs.append(dot(rows_of(2, head), g, NT))
        dv.append(dot(probs[head].astype(jnp.bfloat16), g, NN).astype(jnp.bfloat16))
    dq, dk = [], []
    for head in heads:
        probs_low = probs[head].astype(jnp.bfloat16).astype(jnp.float32)
        row_delta = jnp.sum(probs_low * grad_probs[head], axis=0, keepdims=True)
        grad_scores = (probs[head] * (grad_probs[head] - row_delta)).astype(jnp.bfloat16)
        dk.append((dot(grad_scores, rows_of(0, head), NN) * SCALE).astype(jnp.bfloat16))
        dq.append((dot(rows_of(1, head), grad_scores, TN) * SCALE).astype(jnp.bfloat16))
    send(2, dot(place, jnp.concatenate(dv, axis=1), NN))
    send(1, dot(place, jnp.concatenate(dk, axis=1), NN))
    send(0, dot(place, jnp.concatenate(dq, axis=0), NT))


def pack_kernel(place_ref, x_ref, out_ref):
    ranks, three_rows, width = out_ref.shape
    rows = three_rows // 3
    packed = dot(place_ref[...], x_ref[...], NN).astype(jnp.bfloat16)
    for rank in range(ranks):
        for at in range(3):
            out_ref[rank, at * rows : (at + 1) * rows, :] = packed[
                rank * rows : (rank + 1) * rows, at * width : (at + 1) * width
            ]


def join_kernel(x_ref, q_ref, k_ref, v_ref, whole_ref, sem):
    ranks, three_rows, width = x_ref.shape
    rows = three_rows // 3
    copies = []
    for at, ref in enumerate((q_ref, k_ref, v_ref)):
        for rank in range(ranks):
            whole_ref[at, :, rank * width : (rank + 1) * width] = x_ref[rank, at * rows : (at + 1) * rows, :]
        copies.append(pltpu.make_async_copy(whole_ref.at[at], ref, sem.at[at]))
        copies[-1].start()
    for copy in copies:
        copy.wait()


def whole():
    return pl.BlockSpec(memory_space=pltpu.VMEM)


def scalars():
    return pl.BlockSpec(memory_space=pltpu.SMEM)


def in_place():
    return pl.BlockSpec(memory_space=pl.ANY)


def from_hbm(array):
    return pltpu.with_memory_space_constraint(array, pltpu.HBM)


def local(queries, keys, values, out_grad, lengths, pack_of, source_ids, loss_weights):
    groups = lax.axis_size("dp")
    ranks = lax.axis_size("tensor")
    index = lax.axis_index("dp").astype(jnp.int32).reshape(1)
    rows, feat = queries.shape
    width = feat // ranks
    total = rows * ranks
    slots = groups * PATCH_MAX
    bf16 = jnp.bfloat16

    by_rank = pl.pallas_call(
        split_kernel,
        out_shape=jax.ShapeDtypeStruct((ranks, 4 * rows * (width // HEAD_DIM), HEAD_DIM), bf16),
        in_specs=[in_place()] * 4,
        out_specs=whole(),
        scratch_shapes=[pltpu.VMEM((4, rows, feat), bf16), pltpu.SemaphoreType.DMA((4,))],
        compiler_params=PARAMS,
    )(*(from_hbm(array) for array in (queries, keys, values, out_grad)))
    by_rank, index = lax.optimization_barrier((by_rank, index))
    by_head = lax.all_to_all(by_rank, "tensor", split_axis=0, concat_axis=0, tiled=True)
    same, scale, out_place, in_place_hot = pl.pallas_call(
        index_kernel,
        out_shape=(
            jax.ShapeDtypeStruct((total, total), jnp.float32),
            jax.ShapeDtypeStruct((total, HEAD_DIM), jnp.float32),
            jax.ShapeDtypeStruct((slots, total), bf16),
            jax.ShapeDtypeStruct((total, slots), bf16),
        ),
        in_specs=[scalars(), whole(), whole(), whole(), scalars()],
        out_specs=(whole(),) * 4,
        compiler_params=PARAMS,
        cost_estimate=pl.CostEstimate(flops=1 << 24, bytes_accessed=1 << 20, transcendentals=0),
    )(index, from_hbm(lengths.T), from_hbm(pack_of.T), from_hbm(source_ids.T), loss_weights)
    in_slots = pl.pallas_call(
        grad_kernel,
        out_shape=jax.ShapeDtypeStruct((slots, 3 * width), bf16),
        in_specs=[whole()] * 4,
        out_specs=whole(),
        compiler_params=PARAMS,
    )(same, scale, out_place, by_head)
    arrived = lax.all_to_all(
        in_slots.reshape(groups, PATCH_MAX, 3 * width),
        "dp",
        split_axis=0,
        concat_axis=0,
        axis_index_groups=[[place * STRIDE % groups for place in range(groups)]],
        tiled=True,
    ).reshape(slots, 3 * width)
    packed = pl.pallas_call(
        pack_kernel,
        out_shape=jax.ShapeDtypeStruct((ranks, 3 * rows, width), bf16),
        in_specs=[whole()] * 2,
        out_specs=whole(),
        compiler_params=PARAMS,
    )(in_place_hot, arrived)
    returned = lax.all_to_all(packed, "tensor", split_axis=0, concat_axis=0, tiled=True)
    out = jax.ShapeDtypeStruct((rows, feat), bf16)
    return pl.pallas_call(
        join_kernel,
        out_shape=(out, out, out),
        in_specs=[whole()],
        out_specs=(in_place(), in_place(), in_place()),
        scratch_shapes=[pltpu.VMEM((3, rows, feat), bf16), pltpu.SemaphoreType.DMA((3,))],
        compiler_params=PARAMS,
    )(returned)


def solution(mesh):
    split = P(("dp", "tensor"), None)
    return jax.shard_map(
        local,
        mesh=mesh,
        in_specs=(split,) * 4 + (P(),) * 4,
        out_specs=(split,) * 3,
        check_vma=False,
    )
```

```python
import jax
import jax.numpy as jnp
from jax import lax
from jax.experimental import pallas as pl
from jax.experimental.pallas import tpu as pltpu
from jax.sharding import PartitionSpec as P

HEAD_DIM = 128
PATCH_MAX = 8
MASKED = -1e30
SCALE = HEAD_DIM ** (-0.5)
SCALE_BASE2 = SCALE * 1.4426950408889634

NN = (((1,), (0,)), ((), ()))
NT = (((1,), (1,)), ((), ()))
TN = (((0,), (0,)), ((), ()))

LINE = 8
STRIDE = 29
UNSTRIDE = 53

PARAMS = pltpu.CompilerParams(vmem_limit_bytes=48 * 1024 * 1024)


def dot(a, b, dims):
    return lax.dot_general(a, b, dims, preferred_element_type=jnp.float32)


def iota(shape, axis):
    return lax.broadcasted_iota(jnp.int32, shape, axis)


def low(mask):
    return mask.astype(jnp.float32).astype(jnp.bfloat16)


def turned(index):
    return index % LINE * LINE + index // LINE


def split_kernel(q_ref, k_ref, v_ref, g_ref, out_ref, whole_ref, sem):
    ranks = out_ref.shape[0]
    rows, feat = q_ref.shape
    heads = feat // HEAD_DIM // ranks
    copies = [
        pltpu.make_async_copy(ref, whole_ref.at[at], sem.at[at]) for at, ref in enumerate((q_ref, k_ref, v_ref, g_ref))
    ]
    for copy in copies:
        copy.start()
    for at, copy in enumerate(copies):
        copy.wait()
        for rank in range(ranks):
            for head in range(heads):
                to = (head * 4 + at) * rows
                col = (rank * heads + head) * HEAD_DIM
                out_ref[rank, to : to + rows, :] = whole_ref[at, :, col : col + HEAD_DIM]


def spread_column(column):
    return jnp.broadcast_to(column, (column.shape[0], 128)).astype(jnp.bfloat16)


def index_kernel(
    at_ref, lengths_ref, packs_ref, sources_ref, weights_ref, same_ref, scale_ref, out_place_ref, in_place_ref
):
    images, groups = lengths_ref.shape
    total = same_ref.shape[0]
    slots = groups * PATCH_MAX
    own = at_ref[0]

    lengths, packs = lengths_ref[...], packs_ref[...]
    mine = iota((images, groups), 1) == own
    lens = jnp.sum(jnp.where(mine, lengths, 0).astype(jnp.float32), axis=1, keepdims=True)
    pack = jnp.sum(jnp.where(mine, packs, 0).astype(jnp.float32), axis=1, keepdims=True)
    kind = jnp.sum(jnp.where(mine, sources_ref[...], 0).astype(jnp.float32), axis=1, keepdims=True)

    earlier = iota((images, images), 1) < iota((images, images), 0)
    lens_wide = spread_column(lens)
    starts = dot(low(earlier), lens_wide, NN)[:, 0:1]
    pack_hits = low(iota((images, groups), 1).astype(jnp.float32) == pack)
    same_pack = dot(pack_hits, pack_hits, NT) > 0.5
    prior = dot(low(same_pack & earlier), lens_wide, NN)[:, 0:1]

    row_id = iota((images, total), 1).astype(jnp.float32)
    offset = row_id - starts
    member = (offset >= 0) & (offset < lens)
    member_low = low(member)
    same_ref[...] = jnp.where(dot(member_low, member_low, TN) > 0.5, 0.0, MASKED)

    weight = jnp.zeros((images, 1), jnp.float32)
    for at in range(weights_ref.shape[0]):
        weight = jnp.where(kind == at, weights_ref[at].astype(jnp.float32) * 0.25, weight)
    scale_ref[...] = dot(member_low, spread_column(weight), TN)

    line = jnp.floor(pack * (1.0 / LINE))
    pack = (pack - line * LINE) * LINE + line
    place = pack * UNSTRIDE - jnp.floor(pack * (UNSTRIDE / groups)) * groups
    slot = jnp.sum(jnp.where(member, place * PATCH_MAX + prior + offset + 1.0, 0.0), axis=0, keepdims=True)
    slot = slot.astype(jnp.int32) - 1
    out_place_ref[...] = low(iota((slots, total), 0) == slot)

    arriving = jnp.where(packs == own, lengths, 0).astype(jnp.float32)
    incoming = jnp.broadcast_to(jnp.sum(arriving, axis=0, keepdims=True), (8, groups))
    before = low(iota((groups, groups), 0) < iota((groups, groups), 1))
    begins = dot(incoming.astype(jnp.bfloat16), before, NN)
    to_slots = low(turned(iota((groups, slots), 1) // PATCH_MAX * STRIDE % groups) == iota((groups, slots), 0))
    begin_at = dot(begins.astype(jnp.bfloat16), to_slots, NN)[0:1]
    count_at = dot(incoming.astype(jnp.bfloat16), to_slots, NN)[0:1]
    within = (iota((1, slots), 1) % PATCH_MAX).astype(jnp.float32)
    row = jnp.where(within < count_at, begin_at + within, -1.0).astype(jnp.int32)
    in_place_ref[...] = low(iota((total, slots), 0) == row)


def grad_kernel(same_ref, scale_ref, place_ref, x_ref, out_ref):
    ranks = x_ref.shape[0]
    total = same_ref.shape[0]
    rows = total // ranks
    width = out_ref.shape[1] // 3
    heads = range(width // HEAD_DIM)
    mask = same_ref[...]
    place = place_ref[...]

    def rows_of(at, head):
        begin = (head * 4 + at) * rows
        return x_ref[:, begin : begin + rows, :].reshape(total, HEAD_DIM)

    def send(at, product):
        out_ref[:, at * width : (at + 1) * width] = product.astype(jnp.bfloat16)

    probs, grad_probs, dv = [], [], []
    for head in heads:
        scores = dot(rows_of(1, head), rows_of(0, head), NT) * SCALE_BASE2 + mask
        exp_scores = jnp.exp2(scores - jnp.max(scores, axis=0, keepdims=True))
        probs.append(exp_scores * (1.0 / jnp.sum(exp_scores, axis=0, keepdims=True)))
        g = (rows_of(3, head).astype(jnp.float32) * scale_ref[...]).astype(jnp.bfloat16)
        grad_probs.append(dot(rows_of(2, head), g, NT))
        dv.append(dot(probs[head].astype(jnp.bfloat16), g, NN).astype(jnp.bfloat16))
    dq, dk = [], []
    for head in heads:
        probs_low = probs[head].astype(jnp.bfloat16).astype(jnp.float32)
        row_delta = jnp.sum(probs_low * grad_probs[head], axis=0, keepdims=True)
        grad_scores = (probs[head] * (grad_probs[head] - row_delta)).astype(jnp.bfloat16)
        dk.append((dot(grad_scores, rows_of(0, head), NN) * SCALE).astype(jnp.bfloat16))
        dq.append((dot(rows_of(1, head), grad_scores, TN) * SCALE).astype(jnp.bfloat16))
    send(2, dot(place, jnp.concatenate(dv, axis=1), NN))
    send(1, dot(place, jnp.concatenate(dk, axis=1), NN))
    send(0, dot(place, jnp.concatenate(dq, axis=0), NT))


def pack_kernel(place_ref, x_ref, out_ref):
    ranks, three_rows, width = out_ref.shape
    rows = three_rows // 3
    packed = dot(place_ref[...], x_ref[...], NN).astype(jnp.bfloat16)
    for rank in range(ranks):
        for at in range(3):
            out_ref[rank, at * rows : (at + 1) * rows, :] = packed[
                rank * rows : (rank + 1) * rows, at * width : (at + 1) * width
            ]


def join_kernel(x_ref, q_ref, k_ref, v_ref, whole_ref, sem):
    ranks, three_rows, width = x_ref.shape
    rows = three_rows // 3
    copies = []
    for at, ref in enumerate((q_ref, k_ref, v_ref)):
        for rank in range(ranks):
            whole_ref[at, :, rank * width : (rank + 1) * width] = x_ref[rank, at * rows : (at + 1) * rows, :]
        copies.append(pltpu.make_async_copy(whole_ref.at[at], ref, sem.at[at]))
        copies[-1].start()
    for copy in copies:
        copy.wait()


def whole():
    return pl.BlockSpec(memory_space=pltpu.VMEM)


def scalars():
    return pl.BlockSpec(memory_space=pltpu.SMEM)


def in_place():
    return pl.BlockSpec(memory_space=pl.ANY)


def from_hbm(array):
    return pltpu.with_memory_space_constraint(array, pltpu.HBM)


def local(queries, keys, values, out_grad, lengths, pack_of, source_ids, loss_weights):
    groups = lax.axis_size("dp")
    ranks = lax.axis_size("tensor")
    index = lax.axis_index("dp").astype(jnp.int32).reshape(1)
    rows, feat = queries.shape
    width = feat // ranks
    total = rows * ranks
    slots = groups * PATCH_MAX
    bf16 = jnp.bfloat16

    by_rank = pl.pallas_call(
        split_kernel,
        out_shape=jax.ShapeDtypeStruct((ranks, 4 * rows * (width // HEAD_DIM), HEAD_DIM), bf16),
        in_specs=[in_place()] * 4,
        out_specs=whole(),
        scratch_shapes=[pltpu.VMEM((4, rows, feat), bf16), pltpu.SemaphoreType.DMA((4,))],
        compiler_params=PARAMS,
    )(*(from_hbm(array) for array in (queries, keys, values, out_grad)))
    by_rank, index = lax.optimization_barrier((by_rank, index))
    by_head = lax.all_to_all(by_rank, "tensor", split_axis=0, concat_axis=0, tiled=True)
    same, scale, out_place, in_place_hot = pl.pallas_call(
        index_kernel,
        out_shape=(
            jax.ShapeDtypeStruct((total, total), jnp.float32),
            jax.ShapeDtypeStruct((total, HEAD_DIM), jnp.float32),
            jax.ShapeDtypeStruct((slots, total), bf16),
            jax.ShapeDtypeStruct((total, slots), bf16),
        ),
        in_specs=[scalars(), whole(), whole(), whole(), scalars()],
        out_specs=(whole(),) * 4,
        compiler_params=PARAMS,
        cost_estimate=pl.CostEstimate(flops=1 << 24, bytes_accessed=1 << 20, transcendentals=0),
    )(index, from_hbm(lengths.T), from_hbm(pack_of.T), from_hbm(source_ids.T), loss_weights)
    in_slots = pl.pallas_call(
        grad_kernel,
        out_shape=jax.ShapeDtypeStruct((slots, 3 * width), bf16),
        in_specs=[whole()] * 4,
        out_specs=whole(),
        compiler_params=PARAMS,
    )(same, scale, out_place, by_head)
    arrived = lax.all_to_all(
        in_slots.reshape(groups, PATCH_MAX, 3 * width),
        "dp",
        split_axis=0,
        concat_axis=0,
        axis_index_groups=[[turned(place * STRIDE % groups) for place in range(groups)]],
        tiled=True,
    ).reshape(slots, 3 * width)
    packed = pl.pallas_call(
        pack_kernel,
        out_shape=jax.ShapeDtypeStruct((ranks, 3 * rows, width), bf16),
        in_specs=[whole()] * 2,
        out_specs=whole(),
        compiler_params=PARAMS,
    )(in_place_hot, arrived)
    returned = lax.all_to_all(packed, "tensor", split_axis=0, concat_axis=0, tiled=True)
    out = jax.ShapeDtypeStruct((rows, feat), bf16)
    return pl.pallas_call(
        join_kernel,
        out_shape=(out, out, out),
        in_specs=[whole()],
        out_specs=(in_place(), in_place(), in_place()),
        scratch_shapes=[pltpu.VMEM((3, rows, feat), bf16), pltpu.SemaphoreType.DMA((3,))],
        compiler_params=PARAMS,
    )(returned)


def solution(mesh):
    split = P(("dp", "tensor"), None)
    return jax.shard_map(
        local,
        mesh=mesh,
        in_specs=(split,) * 4 + (P(),) * 4,
        out_specs=(split,) * 3,
        check_vma=False,
    )
```

```python
import jax
import jax.numpy as jnp
from jax import lax
from jax.experimental import pallas as pl
from jax.experimental.pallas import tpu as pltpu
from jax.sharding import PartitionSpec as P

HEAD_DIM = 128
PATCH_MAX = 8
MASKED = -1e30
SCALE = HEAD_DIM ** (-0.5)
SCALE_BASE2 = SCALE * 1.4426950408889634

NN = (((1,), (0,)), ((), ()))
NT = (((1,), (1,)), ((), ()))
TN = (((0,), (0,)), ((), ()))

LINE = 8
STRIDE = 45
UNSTRIDE = 37

PARAMS = pltpu.CompilerParams(vmem_limit_bytes=48 * 1024 * 1024)


def dot(a, b, dims):
    return lax.dot_general(a, b, dims, preferred_element_type=jnp.float32)


def iota(shape, axis):
    return lax.broadcasted_iota(jnp.int32, shape, axis)


def low(mask):
    return mask.astype(jnp.float32).astype(jnp.bfloat16)


def turned(index):
    return index % LINE * LINE + index // LINE


def split_kernel(q_ref, k_ref, v_ref, g_ref, out_ref, whole_ref, sem):
    ranks = out_ref.shape[0]
    rows, feat = q_ref.shape
    heads = feat // HEAD_DIM // ranks
    copies = [
        pltpu.make_async_copy(ref, whole_ref.at[at], sem.at[at]) for at, ref in enumerate((q_ref, k_ref, v_ref, g_ref))
    ]
    for copy in copies:
        copy.start()
    for at, copy in enumerate(copies):
        copy.wait()
        for rank in range(ranks):
            for head in range(heads):
                to = (head * 4 + at) * rows
                col = (rank * heads + head) * HEAD_DIM
                out_ref[rank, to : to + rows, :] = whole_ref[at, :, col : col + HEAD_DIM]


def spread_column(column):
    return jnp.broadcast_to(column, (column.shape[0], 128)).astype(jnp.bfloat16)


def index_kernel(
    at_ref, lengths_ref, packs_ref, sources_ref, weights_ref, same_ref, scale_ref, out_place_ref, in_place_ref
):
    images, groups = lengths_ref.shape
    total = same_ref.shape[0]
    slots = groups * PATCH_MAX
    own = at_ref[0]

    lengths, packs = lengths_ref[...], packs_ref[...]
    mine = iota((images, groups), 1) == own
    lens = jnp.sum(jnp.where(mine, lengths, 0).astype(jnp.float32), axis=1, keepdims=True)
    pack = jnp.sum(jnp.where(mine, packs, 0).astype(jnp.float32), axis=1, keepdims=True)
    kind = jnp.sum(jnp.where(mine, sources_ref[...], 0).astype(jnp.float32), axis=1, keepdims=True)

    earlier = iota((images, images), 1) < iota((images, images), 0)
    lens_wide = spread_column(lens)
    starts = dot(low(earlier), lens_wide, NN)[:, 0:1]
    pack_hits = low(iota((images, groups), 1).astype(jnp.float32) == pack)
    same_pack = dot(pack_hits, pack_hits, NT) > 0.5
    prior = dot(low(same_pack & earlier), lens_wide, NN)[:, 0:1]

    row_id = iota((images, total), 1).astype(jnp.float32)
    offset = row_id - starts
    member = (offset >= 0) & (offset < lens)
    member_low = low(member)
    same_ref[...] = jnp.where(dot(member_low, member_low, TN) > 0.5, 0.0, MASKED)

    weight = jnp.zeros((images, 1), jnp.float32)
    for at in range(weights_ref.shape[0]):
        weight = jnp.where(kind == at, weights_ref[at].astype(jnp.float32) * 0.25, weight)
    scale_ref[...] = dot(member_low, spread_column(weight), TN)

    line = jnp.floor(pack * (1.0 / LINE))
    pack = (pack - line * LINE) * LINE + line
    place = pack * UNSTRIDE - jnp.floor(pack * (UNSTRIDE / groups)) * groups
    slot = jnp.sum(jnp.where(member, place * PATCH_MAX + prior + offset + 1.0, 0.0), axis=0, keepdims=True)
    slot = slot.astype(jnp.int32) - 1
    out_place_ref[...] = low(iota((slots, total), 0) == slot)

    arriving = jnp.where(packs == own, lengths, 0).astype(jnp.float32)
    incoming = jnp.broadcast_to(jnp.sum(arriving, axis=0, keepdims=True), (8, groups))
    before = low(iota((groups, groups), 0) < iota((groups, groups), 1))
    begins = dot(incoming.astype(jnp.bfloat16), before, NN)
    to_slots = low(turned(iota((groups, slots), 1) // PATCH_MAX * STRIDE % groups) == iota((groups, slots), 0))
    begin_at = dot(begins.astype(jnp.bfloat16), to_slots, NN)[0:1]
    count_at = dot(incoming.astype(jnp.bfloat16), to_slots, NN)[0:1]
    within = (iota((1, slots), 1) % PATCH_MAX).astype(jnp.float32)
    row = jnp.where(within < count_at, begin_at + within, -1.0).astype(jnp.int32)
    in_place_ref[...] = low(iota((total, slots), 0) == row)


def grad_kernel(same_ref, scale_ref, place_ref, x_ref, out_ref):
    ranks = x_ref.shape[0]
    total = same_ref.shape[0]
    rows = total // ranks
    width = out_ref.shape[1] // 3
    heads = range(width // HEAD_DIM)
    mask = same_ref[...]
    place = place_ref[...]

    def rows_of(at, head):
        begin = (head * 4 + at) * rows
        return x_ref[:, begin : begin + rows, :].reshape(total, HEAD_DIM)

    def send(at, product):
        out_ref[:, at * width : (at + 1) * width] = product.astype(jnp.bfloat16)

    probs, grad_probs, dv = [], [], []
    for head in heads:
        scores = dot(rows_of(1, head), rows_of(0, head), NT) * SCALE_BASE2 + mask
        exp_scores = jnp.exp2(scores - jnp.max(scores, axis=0, keepdims=True))
        probs.append(exp_scores * (1.0 / jnp.sum(exp_scores, axis=0, keepdims=True)))
        g = (rows_of(3, head).astype(jnp.float32) * scale_ref[...]).astype(jnp.bfloat16)
        grad_probs.append(dot(rows_of(2, head), g, NT))
        dv.append(dot(probs[head].astype(jnp.bfloat16), g, NN).astype(jnp.bfloat16))
    dq, dk = [], []
    for head in heads:
        probs_low = probs[head].astype(jnp.bfloat16).astype(jnp.float32)
        row_delta = jnp.sum(probs_low * grad_probs[head], axis=0, keepdims=True)
        grad_scores = (probs[head] * (grad_probs[head] - row_delta)).astype(jnp.bfloat16)
        dk.append((dot(grad_scores, rows_of(0, head), NN) * SCALE).astype(jnp.bfloat16))
        dq.append((dot(rows_of(1, head), grad_scores, TN) * SCALE).astype(jnp.bfloat16))
    send(2, dot(place, jnp.concatenate(dv, axis=1), NN))
    send(1, dot(place, jnp.concatenate(dk, axis=1), NN))
    send(0, dot(place, jnp.concatenate(dq, axis=0), NT))


def pack_kernel(place_ref, x_ref, out_ref):
    ranks, three_rows, width = out_ref.shape
    rows = three_rows // 3
    packed = dot(place_ref[...], x_ref[...], NN).astype(jnp.bfloat16)
    for rank in range(ranks):
        for at in range(3):
            out_ref[rank, at * rows : (at + 1) * rows, :] = packed[
                rank * rows : (rank + 1) * rows, at * width : (at + 1) * width
            ]


def join_kernel(x_ref, q_ref, k_ref, v_ref, whole_ref, sem):
    ranks, three_rows, width = x_ref.shape
    rows = three_rows // 3
    copies = []
    for at, ref in enumerate((q_ref, k_ref, v_ref)):
        for rank in range(ranks):
            whole_ref[at, :, rank * width : (rank + 1) * width] = x_ref[rank, at * rows : (at + 1) * rows, :]
        copies.append(pltpu.make_async_copy(whole_ref.at[at], ref, sem.at[at]))
        copies[-1].start()
    for copy in copies:
        copy.wait()


def whole():
    return pl.BlockSpec(memory_space=pltpu.VMEM)


def scalars():
    return pl.BlockSpec(memory_space=pltpu.SMEM)


def in_place():
    return pl.BlockSpec(memory_space=pl.ANY)


def from_hbm(array):
    return pltpu.with_memory_space_constraint(array, pltpu.HBM)


def local(queries, keys, values, out_grad, lengths, pack_of, source_ids, loss_weights):
    groups = lax.axis_size("dp")
    ranks = lax.axis_size("tensor")
    index = lax.axis_index("dp").astype(jnp.int32).reshape(1)
    rows, feat = queries.shape
    width = feat // ranks
    total = rows * ranks
    slots = groups * PATCH_MAX
    bf16 = jnp.bfloat16

    by_rank = pl.pallas_call(
        split_kernel,
        out_shape=jax.ShapeDtypeStruct((ranks, 4 * rows * (width // HEAD_DIM), HEAD_DIM), bf16),
        in_specs=[in_place()] * 4,
        out_specs=whole(),
        scratch_shapes=[pltpu.VMEM((4, rows, feat), bf16), pltpu.SemaphoreType.DMA((4,))],
        compiler_params=PARAMS,
    )(*(from_hbm(array) for array in (queries, keys, values, out_grad)))
    by_rank, index = lax.optimization_barrier((by_rank, index))
    by_head = lax.all_to_all(by_rank, "tensor", split_axis=0, concat_axis=0, tiled=True)
    same, scale, out_place, in_place_hot = pl.pallas_call(
        index_kernel,
        out_shape=(
            jax.ShapeDtypeStruct((total, total), jnp.float32),
            jax.ShapeDtypeStruct((total, HEAD_DIM), jnp.float32),
            jax.ShapeDtypeStruct((slots, total), bf16),
            jax.ShapeDtypeStruct((total, slots), bf16),
        ),
        in_specs=[scalars(), whole(), whole(), whole(), scalars()],
        out_specs=(whole(),) * 4,
        compiler_params=PARAMS,
        cost_estimate=pl.CostEstimate(flops=1 << 24, bytes_accessed=1 << 20, transcendentals=0),
    )(index, from_hbm(lengths.T), from_hbm(pack_of.T), from_hbm(source_ids.T), loss_weights)
    in_slots = pl.pallas_call(
        grad_kernel,
        out_shape=jax.ShapeDtypeStruct((slots, 3 * width), bf16),
        in_specs=[whole()] * 4,
        out_specs=whole(),
        compiler_params=PARAMS,
    )(same, scale, out_place, by_head)
    arrived = lax.all_to_all(
        in_slots.reshape(groups, PATCH_MAX, 3 * width),
        "dp",
        split_axis=0,
        concat_axis=0,
        axis_index_groups=[[turned(place * STRIDE % groups) for place in range(groups)]],
        tiled=True,
    ).reshape(slots, 3 * width)
    packed = pl.pallas_call(
        pack_kernel,
        out_shape=jax.ShapeDtypeStruct((ranks, 3 * rows, width), bf16),
        in_specs=[whole()] * 2,
        out_specs=whole(),
        compiler_params=PARAMS,
    )(in_place_hot, arrived)
    returned = lax.all_to_all(packed, "tensor", split_axis=0, concat_axis=0, tiled=True)
    out = jax.ShapeDtypeStruct((rows, feat), bf16)
    return pl.pallas_call(
        join_kernel,
        out_shape=(out, out, out),
        in_specs=[whole()],
        out_specs=(in_place(), in_place(), in_place()),
        scratch_shapes=[pltpu.VMEM((3, rows, feat), bf16), pltpu.SemaphoreType.DMA((3,))],
        compiler_params=PARAMS,
    )(returned)


def solution(mesh):
    split = P(("dp", "tensor"), None)
    return jax.shard_map(
        local,
        mesh=mesh,
        in_specs=(split,) * 4 + (P(),) * 4,
        out_specs=(split,) * 3,
        check_vma=False,
    )
```

```python
import jax
import jax.numpy as jnp
from jax import lax
from jax.experimental import pallas as pl
from jax.experimental.pallas import tpu as pltpu
from jax.sharding import PartitionSpec as P

HEAD_DIM = 128
PATCH_MAX = 8
MASKED = -1e30
SCALE = HEAD_DIM ** (-0.5)
SCALE_BASE2 = SCALE * 1.4426950408889634

NN = (((1,), (0,)), ((), ()))
NT = (((1,), (1,)), ((), ()))
TN = (((0,), (0,)), ((), ()))

LINE = 8
STRIDE = 13
UNSTRIDE = 5

PARAMS = pltpu.CompilerParams(vmem_limit_bytes=48 * 1024 * 1024)


def dot(a, b, dims):
    return lax.dot_general(a, b, dims, preferred_element_type=jnp.float32)


def iota(shape, axis):
    return lax.broadcasted_iota(jnp.int32, shape, axis)


def low(mask):
    return mask.astype(jnp.float32).astype(jnp.bfloat16)


def turned(index):
    return index % LINE * LINE + index // LINE


def split_kernel(q_ref, k_ref, v_ref, g_ref, out_ref, whole_ref, sem):
    ranks = out_ref.shape[0]
    rows, feat = q_ref.shape
    heads = feat // HEAD_DIM // ranks
    copies = [
        pltpu.make_async_copy(ref, whole_ref.at[at], sem.at[at]) for at, ref in enumerate((q_ref, k_ref, v_ref, g_ref))
    ]
    for copy in copies:
        copy.start()
    for at, copy in enumerate(copies):
        copy.wait()
        for rank in range(ranks):
            for head in range(heads):
                to = (head * 4 + at) * rows
                col = (rank * heads + head) * HEAD_DIM
                out_ref[rank, to : to + rows, :] = whole_ref[at, :, col : col + HEAD_DIM]


def spread_column(column):
    return jnp.broadcast_to(column, (column.shape[0], 128)).astype(jnp.bfloat16)


def index_kernel(
    at_ref, lengths_ref, packs_ref, sources_ref, weights_ref, same_ref, scale_ref, out_place_ref, in_place_ref
):
    images, groups = lengths_ref.shape
    total = same_ref.shape[0]
    slots = groups * PATCH_MAX
    own = at_ref[0]

    lengths, packs = lengths_ref[...], packs_ref[...]
    mine = iota((images, groups), 1) == own
    lens = jnp.sum(jnp.where(mine, lengths, 0).astype(jnp.float32), axis=1, keepdims=True)
    pack = jnp.sum(jnp.where(mine, packs, 0).astype(jnp.float32), axis=1, keepdims=True)
    kind = jnp.sum(jnp.where(mine, sources_ref[...], 0).astype(jnp.float32), axis=1, keepdims=True)

    earlier = iota((images, images), 1) < iota((images, images), 0)
    lens_wide = spread_column(lens)
    starts = dot(low(earlier), lens_wide, NN)[:, 0:1]
    pack_hits = low(iota((images, groups), 1).astype(jnp.float32) == pack)
    same_pack = dot(pack_hits, pack_hits, NT) > 0.5
    prior = dot(low(same_pack & earlier), lens_wide, NN)[:, 0:1]

    row_id = iota((images, total), 1).astype(jnp.float32)
    offset = row_id - starts
    member = (offset >= 0) & (offset < lens)
    member_low = low(member)
    same_ref[...] = jnp.where(dot(member_low, member_low, TN) > 0.5, 0.0, MASKED)

    weight = jnp.zeros((images, 1), jnp.float32)
    for at in range(weights_ref.shape[0]):
        weight = jnp.where(kind == at, weights_ref[at].astype(jnp.float32) * 0.25, weight)
    scale_ref[...] = dot(member_low, spread_column(weight), TN)

    line = jnp.floor(pack * (1.0 / LINE))
    pack = (pack - line * LINE) * LINE + line
    place = pack * UNSTRIDE - jnp.floor(pack * (UNSTRIDE / groups)) * groups
    slot = jnp.sum(jnp.where(member, place * PATCH_MAX + prior + offset + 1.0, 0.0), axis=0, keepdims=True)
    slot = slot.astype(jnp.int32) - 1
    out_place_ref[...] = low(iota((slots, total), 0) == slot)

    arriving = jnp.where(packs == own, lengths, 0).astype(jnp.float32)
    incoming = jnp.broadcast_to(jnp.sum(arriving, axis=0, keepdims=True), (8, groups))
    before = low(iota((groups, groups), 0) < iota((groups, groups), 1))
    begins = dot(incoming.astype(jnp.bfloat16), before, NN)
    to_slots = low(turned(iota((groups, slots), 1) // PATCH_MAX * STRIDE % groups) == iota((groups, slots), 0))
    begin_at = dot(begins.astype(jnp.bfloat16), to_slots, NN)[0:1]
    count_at = dot(incoming.astype(jnp.bfloat16), to_slots, NN)[0:1]
    within = (iota((1, slots), 1) % PATCH_MAX).astype(jnp.float32)
    row = jnp.where(within < count_at, begin_at + within, -1.0).astype(jnp.int32)
    in_place_ref[...] = low(iota((total, slots), 0) == row)


def grad_kernel(same_ref, scale_ref, place_ref, x_ref, out_ref):
    ranks = x_ref.shape[0]
    total = same_ref.shape[0]
    rows = total // ranks
    width = out_ref.shape[1] // 3
    heads = range(width // HEAD_DIM)
    mask = same_ref[...]
    place = place_ref[...]

    def rows_of(at, head):
        begin = (head * 4 + at) * rows
        return x_ref[:, begin : begin + rows, :].reshape(total, HEAD_DIM)

    def send(at, product):
        out_ref[:, at * width : (at + 1) * width] = product.astype(jnp.bfloat16)

    probs, grad_probs, dv = [], [], []
    for head in heads:
        scores = dot(rows_of(1, head), rows_of(0, head), NT) * SCALE_BASE2 + mask
        exp_scores = jnp.exp2(scores - jnp.max(scores, axis=0, keepdims=True))
        probs.append(exp_scores * (1.0 / jnp.sum(exp_scores, axis=0, keepdims=True)))
        g = (rows_of(3, head).astype(jnp.float32) * scale_ref[...]).astype(jnp.bfloat16)
        grad_probs.append(dot(rows_of(2, head), g, NT))
        dv.append(dot(probs[head].astype(jnp.bfloat16), g, NN).astype(jnp.bfloat16))
    dq, dk = [], []
    for head in heads:
        probs_low = probs[head].astype(jnp.bfloat16).astype(jnp.float32)
        row_delta = jnp.sum(probs_low * grad_probs[head], axis=0, keepdims=True)
        grad_scores = (probs[head] * (grad_probs[head] - row_delta)).astype(jnp.bfloat16)
        dk.append((dot(grad_scores, rows_of(0, head), NN) * SCALE).astype(jnp.bfloat16))
        dq.append((dot(rows_of(1, head), grad_scores, TN) * SCALE).astype(jnp.bfloat16))
    send(2, dot(place, jnp.concatenate(dv, axis=1), NN))
    send(1, dot(place, jnp.concatenate(dk, axis=1), NN))
    send(0, dot(place, jnp.concatenate(dq, axis=0), NT))


def pack_kernel(place_ref, x_ref, out_ref):
    ranks, three_rows, width = out_ref.shape
    rows = three_rows // 3
    packed = dot(place_ref[...], x_ref[...], NN).astype(jnp.bfloat16)
    for rank in range(ranks):
        for at in range(3):
            out_ref[rank, at * rows : (at + 1) * rows, :] = packed[
                rank * rows : (rank + 1) * rows, at * width : (at + 1) * width
            ]


def join_kernel(x_ref, q_ref, k_ref, v_ref, whole_ref, sem):
    ranks, three_rows, width = x_ref.shape
    rows = three_rows // 3
    copies = []
    for at, ref in enumerate((q_ref, k_ref, v_ref)):
        for rank in range(ranks):
            whole_ref[at, :, rank * width : (rank + 1) * width] = x_ref[rank, at * rows : (at + 1) * rows, :]
        copies.append(pltpu.make_async_copy(whole_ref.at[at], ref, sem.at[at]))
        copies[-1].start()
    for copy in copies:
        copy.wait()


def whole():
    return pl.BlockSpec(memory_space=pltpu.VMEM)


def scalars():
    return pl.BlockSpec(memory_space=pltpu.SMEM)


def in_place():
    return pl.BlockSpec(memory_space=pl.ANY)


def from_hbm(array):
    return pltpu.with_memory_space_constraint(array, pltpu.HBM)


def local(queries, keys, values, out_grad, lengths, pack_of, source_ids, loss_weights):
    groups = lax.axis_size("dp")
    ranks = lax.axis_size("tensor")
    index = lax.axis_index("dp").astype(jnp.int32).reshape(1)
    rows, feat = queries.shape
    width = feat // ranks
    total = rows * ranks
    slots = groups * PATCH_MAX
    bf16 = jnp.bfloat16

    by_rank = pl.pallas_call(
        split_kernel,
        out_shape=jax.ShapeDtypeStruct((ranks, 4 * rows * (width // HEAD_DIM), HEAD_DIM), bf16),
        in_specs=[in_place()] * 4,
        out_specs=whole(),
        scratch_shapes=[pltpu.VMEM((4, rows, feat), bf16), pltpu.SemaphoreType.DMA((4,))],
        compiler_params=PARAMS,
    )(*(from_hbm(array) for array in (queries, keys, values, out_grad)))
    by_rank, index = lax.optimization_barrier((by_rank, index))
    by_head = lax.all_to_all(by_rank, "tensor", split_axis=0, concat_axis=0, tiled=True)
    same, scale, out_place, in_place_hot = pl.pallas_call(
        index_kernel,
        out_shape=(
            jax.ShapeDtypeStruct((total, total), jnp.float32),
            jax.ShapeDtypeStruct((total, HEAD_DIM), jnp.float32),
            jax.ShapeDtypeStruct((slots, total), bf16),
            jax.ShapeDtypeStruct((total, slots), bf16),
        ),
        in_specs=[scalars(), whole(), whole(), whole(), scalars()],
        out_specs=(whole(),) * 4,
        compiler_params=PARAMS,
        cost_estimate=pl.CostEstimate(flops=1 << 24, bytes_accessed=1 << 20, transcendentals=0),
    )(index, from_hbm(lengths.T), from_hbm(pack_of.T), from_hbm(source_ids.T), loss_weights)
    in_slots = pl.pallas_call(
        grad_kernel,
        out_shape=jax.ShapeDtypeStruct((slots, 3 * width), bf16),
        in_specs=[whole()] * 4,
        out_specs=whole(),
        compiler_params=PARAMS,
    )(same, scale, out_place, by_head)
    arrived = lax.all_to_all(
        in_slots.reshape(groups, PATCH_MAX, 3 * width),
        "dp",
        split_axis=0,
        concat_axis=0,
        axis_index_groups=[[turned(place * STRIDE % groups) for place in range(groups)]],
        tiled=True,
    ).reshape(slots, 3 * width)
    packed = pl.pallas_call(
        pack_kernel,
        out_shape=jax.ShapeDtypeStruct((ranks, 3 * rows, width), bf16),
        in_specs=[whole()] * 2,
        out_specs=whole(),
        compiler_params=PARAMS,
    )(in_place_hot, arrived)
    returned = lax.all_to_all(packed, "tensor", split_axis=0, concat_axis=0, tiled=True)
    out = jax.ShapeDtypeStruct((rows, feat), bf16)
    return pl.pallas_call(
        join_kernel,
        out_shape=(out, out, out),
        in_specs=[whole()],
        out_specs=(in_place(), in_place(), in_place()),
        scratch_shapes=[pltpu.VMEM((3, rows, feat), bf16), pltpu.SemaphoreType.DMA((3,))],
        compiler_params=PARAMS,
    )(returned)


def solution(mesh):
    split = P(("dp", "tensor"), None)
    return jax.shard_map(
        local,
        mesh=mesh,
        in_specs=(split,) * 4 + (P(),) * 4,
        out_specs=(split,) * 3,
        check_vma=False,
    )
```

```python
import jax
import jax.numpy as jnp
from jax import lax
from jax.experimental import pallas as pl
from jax.experimental.pallas import tpu as pltpu
from jax.sharding import PartitionSpec as P

HEAD_DIM = 128
PATCH_MAX = 8
MASKED = -1e30
SCALE = HEAD_DIM ** (-0.5)
SCALE_BASE2 = SCALE * 1.4426950408889634

NN = (((1,), (0,)), ((), ()))
NT = (((1,), (1,)), ((), ()))
TN = (((0,), (0,)), ((), ()))

LINE = 8
STRIDE = 27
UNSTRIDE = 19

PARAMS = pltpu.CompilerParams(vmem_limit_bytes=48 * 1024 * 1024)


def dot(a, b, dims):
    return lax.dot_general(a, b, dims, preferred_element_type=jnp.float32)


def iota(shape, axis):
    return lax.broadcasted_iota(jnp.int32, shape, axis)


def low(mask):
    return mask.astype(jnp.float32).astype(jnp.bfloat16)


def turned(index):
    return index % LINE * LINE + index // LINE


def split_kernel(q_ref, k_ref, v_ref, g_ref, out_ref, whole_ref, sem):
    ranks = out_ref.shape[0]
    rows, feat = q_ref.shape
    heads = feat // HEAD_DIM // ranks
    copies = [
        pltpu.make_async_copy(ref, whole_ref.at[at], sem.at[at]) for at, ref in enumerate((q_ref, k_ref, v_ref, g_ref))
    ]
    for copy in copies:
        copy.start()
    for at, copy in enumerate(copies):
        copy.wait()
        for rank in range(ranks):
            for head in range(heads):
                to = (head * 4 + at) * rows
                col = (rank * heads + head) * HEAD_DIM
                out_ref[rank, to : to + rows, :] = whole_ref[at, :, col : col + HEAD_DIM]


def spread_column(column):
    return jnp.broadcast_to(column, (column.shape[0], 128)).astype(jnp.bfloat16)


def index_kernel(
    at_ref, lengths_ref, packs_ref, sources_ref, weights_ref, same_ref, scale_ref, out_place_ref, in_place_ref
):
    images, groups = lengths_ref.shape
    total = same_ref.shape[0]
    slots = groups * PATCH_MAX
    own = at_ref[0]

    lengths, packs = lengths_ref[...], packs_ref[...]
    mine = iota((images, groups), 1) == own
    lens = jnp.sum(jnp.where(mine, lengths, 0).astype(jnp.float32), axis=1, keepdims=True)
    pack = jnp.sum(jnp.where(mine, packs, 0).astype(jnp.float32), axis=1, keepdims=True)
    kind = jnp.sum(jnp.where(mine, sources_ref[...], 0).astype(jnp.float32), axis=1, keepdims=True)

    earlier = iota((images, images), 1) < iota((images, images), 0)
    lens_wide = spread_column(lens)
    starts = dot(low(earlier), lens_wide, NN)[:, 0:1]
    pack_hits = low(iota((images, groups), 1).astype(jnp.float32) == pack)
    same_pack = dot(pack_hits, pack_hits, NT) > 0.5
    prior = dot(low(same_pack & earlier), lens_wide, NN)[:, 0:1]

    row_id = iota((images, total), 1).astype(jnp.float32)
    offset = row_id - starts
    member = (offset >= 0) & (offset < lens)
    member_low = low(member)
    same_ref[...] = jnp.where(dot(member_low, member_low, TN) > 0.5, 0.0, MASKED)

    weight = jnp.zeros((images, 1), jnp.float32)
    for at in range(weights_ref.shape[0]):
        weight = jnp.where(kind == at, weights_ref[at].astype(jnp.float32) * 0.25, weight)
    scale_ref[...] = dot(member_low, spread_column(weight), TN)

    line = jnp.floor(pack * (1.0 / LINE))
    pack = (pack - line * LINE) * LINE + line
    place = pack * UNSTRIDE - jnp.floor(pack * (UNSTRIDE / groups)) * groups
    slot = jnp.sum(jnp.where(member, place * PATCH_MAX + prior + offset + 1.0, 0.0), axis=0, keepdims=True)
    slot = slot.astype(jnp.int32) - 1
    out_place_ref[...] = low(iota((slots, total), 0) == slot)

    arriving = jnp.where(packs == own, lengths, 0).astype(jnp.float32)
    incoming = jnp.broadcast_to(jnp.sum(arriving, axis=0, keepdims=True), (8, groups))
    before = low(iota((groups, groups), 0) < iota((groups, groups), 1))
    begins = dot(incoming.astype(jnp.bfloat16), before, NN)
    to_slots = low(turned(iota((groups, slots), 1) // PATCH_MAX * STRIDE % groups) == iota((groups, slots), 0))
    begin_at = dot(begins.astype(jnp.bfloat16), to_slots, NN)[0:1]
    count_at = dot(incoming.astype(jnp.bfloat16), to_slots, NN)[0:1]
    within = (iota((1, slots), 1) % PATCH_MAX).astype(jnp.float32)
    row = jnp.where(within < count_at, begin_at + within, -1.0).astype(jnp.int32)
    in_place_ref[...] = low(iota((total, slots), 0) == row)


def grad_kernel(same_ref, scale_ref, place_ref, x_ref, out_ref):
    ranks = x_ref.shape[0]
    total = same_ref.shape[0]
    rows = total // ranks
    width = out_ref.shape[1] // 3
    heads = range(width // HEAD_DIM)
    mask = same_ref[...]
    place = place_ref[...]

    def rows_of(at, head):
        begin = (head * 4 + at) * rows
        return x_ref[:, begin : begin + rows, :].reshape(total, HEAD_DIM)

    def send(at, product):
        out_ref[:, at * width : (at + 1) * width] = product.astype(jnp.bfloat16)

    probs, grad_probs, dv = [], [], []
    for head in heads:
        scores = dot(rows_of(1, head), rows_of(0, head), NT) * SCALE_BASE2 + mask
        exp_scores = jnp.exp2(scores - jnp.max(scores, axis=0, keepdims=True))
        probs.append(exp_scores * (1.0 / jnp.sum(exp_scores, axis=0, keepdims=True)))
        g = (rows_of(3, head).astype(jnp.float32) * scale_ref[...]).astype(jnp.bfloat16)
        grad_probs.append(dot(rows_of(2, head), g, NT))
        dv.append(dot(probs[head].astype(jnp.bfloat16), g, NN).astype(jnp.bfloat16))
    dq, dk = [], []
    for head in heads:
        probs_low = probs[head].astype(jnp.bfloat16).astype(jnp.float32)
        row_delta = jnp.sum(probs_low * grad_probs[head], axis=0, keepdims=True)
        grad_scores = (probs[head] * (grad_probs[head] - row_delta)).astype(jnp.bfloat16)
        dk.append((dot(grad_scores, rows_of(0, head), NN) * SCALE).astype(jnp.bfloat16))
        dq.append((dot(rows_of(1, head), grad_scores, TN) * SCALE).astype(jnp.bfloat16))
    send(2, dot(place, jnp.concatenate(dv, axis=1), NN))
    send(1, dot(place, jnp.concatenate(dk, axis=1), NN))
    send(0, dot(place, jnp.concatenate(dq, axis=0), NT))


def pack_kernel(place_ref, x_ref, out_ref):
    ranks, three_rows, width = out_ref.shape
    rows = three_rows // 3
    packed = dot(place_ref[...], x_ref[...], NN).astype(jnp.bfloat16)
    for rank in range(ranks):
        for at in range(3):
            out_ref[rank, at * rows : (at + 1) * rows, :] = packed[
                rank * rows : (rank + 1) * rows, at * width : (at + 1) * width
            ]


def join_kernel(x_ref, q_ref, k_ref, v_ref, whole_ref, sem):
    ranks, three_rows, width = x_ref.shape
    rows = three_rows // 3
    copies = []
    for at, ref in enumerate((q_ref, k_ref, v_ref)):
        for rank in range(ranks):
            whole_ref[at, :, rank * width : (rank + 1) * width] = x_ref[rank, at * rows : (at + 1) * rows, :]
        copies.append(pltpu.make_async_copy(whole_ref.at[at], ref, sem.at[at]))
        copies[-1].start()
    for copy in copies:
        copy.wait()


def whole():
    return pl.BlockSpec(memory_space=pltpu.VMEM)


def scalars():
    return pl.BlockSpec(memory_space=pltpu.SMEM)


def in_place():
    return pl.BlockSpec(memory_space=pl.ANY)


def from_hbm(array):
    return pltpu.with_memory_space_constraint(array, pltpu.HBM)


def local(queries, keys, values, out_grad, lengths, pack_of, source_ids, loss_weights):
    groups = lax.axis_size("dp")
    ranks = lax.axis_size("tensor")
    index = lax.axis_index("dp").astype(jnp.int32).reshape(1)
    rows, feat = queries.shape
    width = feat // ranks
    total = rows * ranks
    slots = groups * PATCH_MAX
    bf16 = jnp.bfloat16

    by_rank = pl.pallas_call(
        split_kernel,
        out_shape=jax.ShapeDtypeStruct((ranks, 4 * rows * (width // HEAD_DIM), HEAD_DIM), bf16),
        in_specs=[in_place()] * 4,
        out_specs=whole(),
        scratch_shapes=[pltpu.VMEM((4, rows, feat), bf16), pltpu.SemaphoreType.DMA((4,))],
        compiler_params=PARAMS,
    )(*(from_hbm(array) for array in (queries, keys, values, out_grad)))
    by_rank, index = lax.optimization_barrier((by_rank, index))
    by_head = lax.all_to_all(by_rank, "tensor", split_axis=0, concat_axis=0, tiled=True)
    same, scale, out_place, in_place_hot = pl.pallas_call(
        index_kernel,
        out_shape=(
            jax.ShapeDtypeStruct((total, total), jnp.float32),
            jax.ShapeDtypeStruct((total, HEAD_DIM), jnp.float32),
            jax.ShapeDtypeStruct((slots, total), bf16),
            jax.ShapeDtypeStruct((total, slots), bf16),
        ),
        in_specs=[scalars(), whole(), whole(), whole(), scalars()],
        out_specs=(whole(),) * 4,
        compiler_params=PARAMS,
        cost_estimate=pl.CostEstimate(flops=1 << 24, bytes_accessed=1 << 20, transcendentals=0),
    )(index, from_hbm(lengths.T), from_hbm(pack_of.T), from_hbm(source_ids.T), loss_weights)
    in_slots = pl.pallas_call(
        grad_kernel,
        out_shape=jax.ShapeDtypeStruct((slots, 3 * width), bf16),
        in_specs=[whole()] * 4,
        out_specs=whole(),
        compiler_params=PARAMS,
    )(same, scale, out_place, by_head)
    arrived = lax.all_to_all(
        in_slots.reshape(groups, PATCH_MAX, 3 * width),
        "dp",
        split_axis=0,
        concat_axis=0,
        axis_index_groups=[[turned(place * STRIDE % groups) for place in range(groups)]],
        tiled=True,
    ).reshape(slots, 3 * width)
    packed = pl.pallas_call(
        pack_kernel,
        out_shape=jax.ShapeDtypeStruct((ranks, 3 * rows, width), bf16),
        in_specs=[whole()] * 2,
        out_specs=whole(),
        compiler_params=PARAMS,
    )(in_place_hot, arrived)
    returned = lax.all_to_all(packed, "tensor", split_axis=0, concat_axis=0, tiled=True)
    out = jax.ShapeDtypeStruct((rows, feat), bf16)
    return pl.pallas_call(
        join_kernel,
        out_shape=(out, out, out),
        in_specs=[whole()],
        out_specs=(in_place(), in_place(), in_place()),
        scratch_shapes=[pltpu.VMEM((3, rows, feat), bf16), pltpu.SemaphoreType.DMA((3,))],
        compiler_params=PARAMS,
    )(returned)


def solution(mesh):
    split = P(("dp", "tensor"), None)
    return jax.shard_map(
        local,
        mesh=mesh,
        in_specs=(split,) * 4 + (P(),) * 4,
        out_specs=(split,) * 3,
        check_vma=False,
    )
```
